128 devices in a mesh: src: 16 (over y_lo, z, core), snk: 8 (over x, y_hi).
Axes of the slice: x: 4, y: 4 (y_hi: 2, y_lo: 2; y = y_hi * 2 + y_lo), z: 4, core: 2. Of those that a mesh axis runs over, the one named last changes fastest.
Arguments:
- perambulators: bfloat16 [16, 16, 2, 512, 512], P('src'), may hold values from -2 to 2, as said below
- elements: bfloat16 [16, 8, 2, 512, 512], P('src', None, None, 'snk'), may hold values from -0.25 to 0.25
Outputs:
- correlator: float32 [2, 16, 16, 8, 8], P(None, 'src', 'snk')
The draws below stay inside these ranges and needn't reach their ends.
Inputs may be any that keep to these rules, and one draw needn't show every extreme that they name: For all times x, y: perambulators[x, y] = Q(y<-x), i.e.
All inputs are finite; a program needn't handle non-finite values.
Results may differ from the reference program's by a relative error of at most 0.0041.
Values may be sent and summed in bfloat16 or wider, within the bound.
A program may use at most 128 MiB of HBM per device.

```python
import jax
import jax.numpy as jnp
from jax import lax

V = 512
OPS = 8
NT = 16


def draw_perambulators(key, part):
    key = jax.random.fold_in(key, 11)
    shape = (NT, NT, 2, V, V)
    base = jnp.clip(jax.random.normal(key, shape, jnp.float32), -6.0, 6.0)
    base = base * V ** (-0.5)
    index = lax.iota(jnp.int32, V)
    signs = jnp.where(index < V // 2, 1.0, -1.0).astype(jnp.float32)
    weight = signs[:, None] * signs[None, :]
    swapped = jnp.swapaxes(jnp.swapaxes(base, 0, 1), 3, 4)
    conjugate = jnp.stack([swapped[:, :, 0], -swapped[:, :, 1]], axis=2)
    image = weight * conjugate
    source_idx = jnp.arange(NT, dtype=jnp.int32)[:, None]
    sink_idx = jnp.arange(NT, dtype=jnp.int32)[None, :]
    separation = (sink_idx - source_idx) % NT
    keep_base = (separation < NT // 2) | (separation == NT // 2) & (source_idx < NT // 2)
    keep_base = keep_base & (separation != 0)
    diagonal = (separation == 0)[:, :, None, None, None]
    mixed = jnp.where(keep_base[:, :, None, None, None], base, image)
    mixed = jnp.where(diagonal, (base + image) * 0.70710678, mixed)
    return mixed.astype(jnp.bfloat16)


def block_levels(key, shape, shards, smallest, largest):
    def one(dim, shards_of):
        steps = jax.random.uniform(jax.random.fold_in(jax.random.fold_in(key, 6), dim), (shards_of,), jnp.float32, smallest / len(shards), largest / len(shards))
        return jnp.repeat(jnp.exp(steps), shape[dim] // shards_of).reshape((-1,) + (1,) * (len(shape) - dim - 1))

    level = one(*shards[0])
    for cut in shards[1:]:
        level = level * one(*cut)
    return level


def scatter_about(stream_key, shape, spread, bound, shards=(), held_as=jnp.bfloat16):
    array = jax.random.normal(stream_key, shape, jnp.float32) * spread
    if len(shards) > 0:
        array = block_levels(stream_key, shape, shards, -0.22, 0.18) * array
    return jnp.clip(array, min=-bound, max=bound).astype(held_as)


def setup_inputs(seed: int = 0) -> dict:
    splits = jax.random.split(jax.random.key(seed), 3)
    perambulators = draw_perambulators(jax.random.fold_in(splits[2], 71), 0)
    elements = scatter_about(splits[1], (NT, OPS, 2, V, V), V ** -0.5, 0.25, ((0, 16), (3, 8)))
    return dict(perambulators=perambulators, elements=elements)


def spin_sign(size, count):
    index = lax.iota(jnp.int32, count)
    return jnp.where(index < size // 2, 1.0, -1.0).astype(jnp.float32)


def pair_traces(sink_full, perambulator, source_full):
    width = perambulator.shape[-1]
    s_real = sink_full[:, 0].astype(jnp.float32)
    s_imag = sink_full[:, 1].astype(jnp.float32)
    t_real = perambulator[0].astype(jnp.float32)
    t_imag = perambulator[1].astype(jnp.float32)
    b_real = (jnp.einsum('orv,vw->orw', s_real, t_real) - jnp.einsum('orv,vw->orw', s_imag, t_imag)).astype(jnp.bfloat16)
    b_imag = (jnp.einsum('orv,vw->orw', s_real, t_imag) + jnp.einsum('orv,vw->orw', s_imag, t_real)).astype(jnp.bfloat16)
    signs = spin_sign(width, width)
    weight = signs[:, None] * signs[None, :]
    m_real = weight * t_real
    m_imag = -(weight * t_imag)
    u_real = source_full[:, 0].astype(jnp.float32)
    u_imag = source_full[:, 1].astype(jnp.float32)
    a_real = (jnp.einsum('ik,ojk->oij', m_real, u_real) - jnp.einsum('ik,ojk->oij', m_imag, u_imag)).astype(jnp.bfloat16)
    a_imag = (jnp.einsum('ik,ojk->oij', m_real, u_imag) + jnp.einsum('ik,ojk->oij', m_imag, u_real)).astype(jnp.bfloat16)
    count = b_real.shape[0]
    flat_br = b_real.reshape(count, -1).astype(jnp.float32)
    flat_bi = b_imag.reshape(count, -1).astype(jnp.float32)
    flat_ar = a_real.reshape(count, -1).astype(jnp.float32)
    flat_ai = a_imag.reshape(count, -1).astype(jnp.float32)
    c_real = jnp.einsum('an,bn->ab', flat_br, flat_ar) - jnp.einsum('an,bn->ab', flat_bi, flat_ai)
    c_imag = jnp.einsum('an,bn->ab', flat_br, flat_ai) + jnp.einsum('an,bn->ab', flat_bi, flat_ar)
    return jnp.stack([c_real, c_imag])


def reference(perambulators, elements):
    half_cycle = NT // 2

    def per_source(source):
        peram_row = lax.dynamic_index_in_dim(perambulators, source, 0, keepdims=False)
        source_full = lax.dynamic_index_in_dim(elements, source, 0, keepdims=False)
        values = []
        for distance in range(half_cycle + 1):
            target = ((source + distance) % NT).astype(jnp.int32)
            sink_full = lax.dynamic_index_in_dim(elements, target, 0, keepdims=False)
            peram = lax.dynamic_index_in_dim(peram_row, target, 0, keepdims=False)
            values.append(pair_traces(sink_full, peram, source_full))
        return jnp.stack(values)

    direct = lax.map(per_source, jnp.arange(NT, dtype=jnp.int32))
    source_idx = jnp.arange(NT, dtype=jnp.int32)[:, None]
    sink_idx = jnp.arange(NT, dtype=jnp.int32)[None, :]
    forward = (sink_idx - source_idx) % NT
    backward = (source_idx - sink_idx) % NT
    owned = (forward < half_cycle) | ((forward == half_cycle) & (source_idx < half_cycle))
    straight = direct[source_idx, jnp.minimum(forward, half_cycle)]
    swapped = jnp.swapaxes(direct[sink_idx, jnp.minimum(backward, half_cycle)], -1, -2)
    combined = jnp.where(owned[:, :, None, None, None], straight, swapped)
    return jnp.transpose(combined, (2, 0, 1, 3, 4))
```

```python
import jax
import jax.numpy as jnp
from jax import lax
from jax.experimental import pallas as pl
from jax.experimental.pallas import tpu as pltpu
from jax.sharding import PartitionSpec as P

MESH = pl.DeviceIdType.MESH
UNITS = 9
NT_DIMS = (((1,), (1,)), ((), ()))

FLIP, NEXT, FLIP_PREV, HALF = 0, 1, 2, 3
SIB_OWN, SIB_FLIP, SIB_NEXT, SIB_FLIP_PREV, SIB_HALF = 4, 5, 6, 7, 8


def dot(a, b):
    return jnp.dot(a, b, preferred_element_type=jnp.float32)


def dot_nt(a, b):
    return lax.dot_general(a, b, NT_DIMS, preferred_element_type=jnp.float32)


def exact_nt(a, b):
    return lax.dot_general(
        a, b, NT_DIMS, preferred_element_type=jnp.float32, precision=lax.Precision.HIGHEST
    )


def kernel(
    peram, elem, out, full, other, mats, left, xs, ys, parts, sums, swapped,
    load_sem, send_sem, recv_sem, part_send, part_recv, swap_send, swap_recv,
):
    src = lax.axis_index("src")
    snk = lax.axis_index("snk")
    core = lax.rem(src, 2)
    z = lax.rem(src // 2, 4)
    ylo = src // 8
    x = snk // 2
    yhi = lax.rem(snk, 2)
    y = yhi * 2 + ylo
    tau = src // 2
    ops = elem.shape[1]
    rows = elem.shape[3]

    def place(px, py, pz, pc):
        return ((lax.rem(py, 2) * 4 + pz) * 2 + pc, px * 2 + py // 2)

    xr = lax.rem(x + 1, 4)
    xl = lax.rem(x + 3, 4)
    xo = lax.rem(x + 2, 4)
    yn = lax.rem(y + 1, 4)
    yp = lax.rem(y + 3, 4)
    yo = lax.rem(y + 2, 4)
    zn = lax.rem(z + 1, 4)
    zp = lax.rem(z + 3, 4)
    zo = lax.rem(z + 2, 4)
    yoh = yo // 2
    dev_xr = place(xr, y, z, core)
    dev_xl = place(xl, y, z, core)
    dev_yo = place(x, yo, z, core)
    y_to = lax.rem(y + 3 + 2 * core, 4)
    y_from = lax.rem(y + 1 + 2 * core, 4)
    y_from_sib = lax.rem(y + 3 + 2 * core, 4)
    dev_flip = place(x, y_to, z, core)
    dev_flip_back = place(x, y_from, z, core)
    dev_zn = place(x, y, zn, core)
    dev_zp = place(x, y, zp, core)
    dev_zo = place(x, y, zo, core)
    dev_sib = (src + 1 - 2 * core, snk)

    own_rows = snk
    flip_rows = x * 2 + y_from // 2
    flip_rows_sib = x * 2 + y_from_sib // 2
    low = z < 2
    flip_tau = (1 - ylo) * 4 + z
    next_tau = ylo * 4 + zn
    prev_tau = (1 - ylo) * 4 + zp
    half_tau = jnp.where(low, ylo, 1 - ylo) * 4 + zo
    sib = 1 - core
    flip_core = lax.rem(core + ylo, 2)
    taus = [tau, tau, flip_tau, next_tau, next_tau, prev_tau, prev_tau, half_tau, half_tau]
    cores = [core, sib, flip_core, core, sib, core, sib, core, sib]
    blocks = [
        own_rows,
        own_rows,
        jnp.where(ylo == 0, flip_rows, flip_rows_sib),
        own_rows,
        own_rows,
        flip_rows,
        flip_rows_sib,
        jnp.where(low, own_rows, flip_rows),
        jnp.where(low, own_rows, flip_rows_sib),
    ]
    slots = [
        None, SIB_OWN, jnp.where(ylo == 0, FLIP, SIB_FLIP), NEXT, SIB_NEXT,
        FLIP_PREV, SIB_FLIP_PREV, HALF, SIB_HALF,
    ]

    own_slice = full.at[:, :, pl.ds(pl.multiple_of(snk * rows, rows), rows), :]
    own_load = pltpu.make_async_copy(elem.at[0], own_slice, load_sem.at[UNITS])
    own_load.start()
    loads = []
    for u in range(UNITS):
        load = pltpu.make_async_copy(
            peram.at[0, taus[u] * 2 + cores[u]], mats.at[u], load_sem.at[u]
        )
        load.start()
        loads.append(load)

    swapped[...] = jnp.zeros_like(swapped)

    barrier = pltpu.get_barrier_semaphore()
    for step in range(1, 8):
        pl.semaphore_signal(
            barrier, inc=1, device_id=(src, lax.rem(snk + step, 8)), device_id_type=MESH
        )
    for target in (dev_flip, dev_flip_back, dev_zn, dev_zp, dev_zo, dev_sib):
        pl.semaphore_signal(barrier, inc=1, device_id=target, device_id_type=MESH)
    outside = snk != tau

    @pl.when(outside)
    def _():
        for c in range(2):
            pl.semaphore_signal(barrier, inc=1, device_id=(snk * 2 + c, tau), device_id_type=MESH)

    pl.semaphore_wait(barrier, jnp.where(outside, 15, 13))

    sent = []
    counter = [0]

    def remote(source, target, device):
        k = counter[0]
        counter[0] += 1
        copy = pltpu.make_async_remote_copy(
            src_ref=source, dst_ref=target, send_sem=send_sem.at[k], recv_sem=recv_sem.at[k],
            device_id=device, device_id_type=MESH,
        )
        copy.start()
        sent.append(copy)
        return k

    def arrived(k, target):
        pltpu.make_async_remote_copy(
            src_ref=target, dst_ref=target, send_sem=send_sem.at[k], recv_sem=recv_sem.at[k],
            device_id=dev_sib, device_id_type=MESH,
        ).wait_recv()

    def rows_of(px, pyh, first=0, count=ops):
        start = pl.multiple_of((px * 2 + pyh) * rows, rows)
        return full.at[pl.ds(first, count), :, pl.ds(start, rows), :]

    mine = elem.at[0]
    half = ops // 2
    k_flip = remote(mine, other.at[FLIP], dev_flip)
    k_xr = remote(mine, rows_of(x, yhi), dev_xr)
    k_xl = remote(mine, rows_of(x, yhi), dev_xl)
    k_yo = remote(mine, rows_of(x, yhi), dev_yo)
    k_next = remote(mine, other.at[NEXT], dev_zp)
    k_sib = remote(mine, other.at[SIB_OWN], dev_sib)

    col = lax.broadcasted_iota(jnp.int32, (rows, 512), 1)
    lane_sign = jnp.where(col < 256, 1.0, -1.0) * jnp.where(x < 2, 1.0, -1.0)

    def prepare(u):
        loads[u].wait()
        start = pl.multiple_of(blocks[u] * rows, rows)
        re = mats[u, 0, pl.ds(start, rows), :].astype(jnp.float32) * lane_sign
        im = mats[u, 1, pl.ds(start, rows), :].astype(jnp.float32) * lane_sign
        left[0, u, 0] = re.astype(jnp.bfloat16)
        left[0, u, 1] = (-im).astype(jnp.bfloat16)
        left[1, u, 0] = im.astype(jnp.bfloat16)
        left[1, u, 1] = re.astype(jnp.bfloat16)

    def sink_product(u):
        prepare(u)

        def tile(n, carry):
            cols = pl.ds(pl.multiple_of(n * 256, 256), 256)
            if u == 0:
                start = pl.multiple_of(snk * rows, rows)
                er = full[:, 0, pl.ds(start, rows), :]
                ei = full[:, 1, pl.ds(start, rows), :]
            else:
                er = other[slots[u], :, 0]
                ei = other[slots[u], :, 1]
            er = er.reshape(ops * rows, 512)
            ei = ei.reshape(ops * rows, 512)
            pr = mats[u, 0, :, cols]
            pi = mats[u, 1, :, cols]
            re = dot(er, pr) - dot(ei, pi)
            im = dot(er, pi) + dot(ei, pr)
            xs[u, 0, :, :, cols] = re.astype(jnp.bfloat16).reshape(ops, rows, 256)
            xs[u, 1, :, :, cols] = im.astype(jnp.bfloat16).reshape(ops, rows, 256)
            return carry

        lax.fori_loop(0, 2, tile, 0)

    def source_product(px):
        cols = pl.ds(pl.multiple_of(px * 128, 128), 128)

        def tile(q, carry):
            o = q * 2
            wr = full[pl.ds(o, 2), 0, cols, :].reshape(256, 512)
            wi = full[pl.ds(o, 2), 1, cols, :].reshape(256, 512)
            for m in range(3):
                a = left[0, 3 * m : 3 * m + 3].reshape(384, 512)
                b = left[1, 3 * m : 3 * m + 3].reshape(384, 512)
                r = (dot_nt(a, wr) + dot_nt(b, wi)).astype(jnp.bfloat16)
                ys[3 * m : 3 * m + 3, :, o, :, cols] = r[:, :128].reshape(3, 2, rows, 128)
                ys[3 * m : 3 * m + 3, :, o + 1, :, cols] = r[:, 128:].reshape(3, 2, rows, 128)
            return carry

        lax.fori_loop(0, ops // 2, tile, 0)

    own_load.wait()
    sink_product(0)
    arrived(k_flip, other.at[FLIP])
    k_prev = remote(other.at[FLIP], other.at[FLIP_PREV], dev_zn)
    k_half = counter[0]
    counter[0] += 1

    def half_copy(source):
        return pltpu.make_async_remote_copy(
            src_ref=source, dst_ref=other.at[HALF], send_sem=send_sem.at[k_half],
            recv_sem=recv_sem.at[k_half], device_id=dev_zo, device_id_type=MESH,
        )

    @pl.when(low)
    def _():
        half_copy(other.at[FLIP]).start()

    @pl.when(jnp.logical_not(low))
    def _():
        half_copy(mine).start()

    k_sib_flip = remote(other.at[FLIP], other.at[SIB_FLIP], dev_sib)
    arrived(k_sib, other.at[SIB_OWN])
    sink_product(1)
    arrived(k_sib_flip, other.at[SIB_FLIP])
    sink_product(2)

    def forward(k_from_left, k_from_right, pyh):
        arrived(k_from_left, rows_of(xl, pyh))
        on_right = remote(rows_of(xl, pyh, half, half), rows_of(xl, pyh, half, half), dev_xr)
        arrived(k_from_right, rows_of(xr, pyh))
        on_left = remote(rows_of(xr, pyh, 0, half), rows_of(xr, pyh, 0, half), dev_xl)
        return on_right, on_left

    own_right, own_left = forward(k_xr, k_xl, yhi)
    arrived(k_yo, rows_of(x, yoh))
    k_oxr = remote(rows_of(x, yoh), rows_of(x, yoh), dev_xr)
    k_oxl = remote(rows_of(x, yoh), rows_of(x, yoh), dev_xl)
    arrived(k_next, other.at[NEXT])
    k_sib_next = remote(other.at[NEXT], other.at[SIB_NEXT], dev_sib)
    sink_product(3)
    arrived(k_sib_next, other.at[SIB_NEXT])
    sink_product(4)
    arrived(k_prev, other.at[FLIP_PREV])
    k_sib_prev = remote(other.at[FLIP_PREV], other.at[SIB_FLIP_PREV], dev_sib)
    sink_product(5)
    arrived(k_sib_prev, other.at[SIB_FLIP_PREV])
    sink_product(6)
    arrived(k_half, other.at[HALF])
    k_sib_half = remote(other.at[HALF], other.at[SIB_HALF], dev_sib)
    sink_product(7)
    arrived(k_sib_half, other.at[SIB_HALF])
    sink_product(8)
    source_product(x)
    other_right, other_left = forward(k_oxr, k_oxl, yoh)
    source_product(xl)
    source_product(xr)
    for k_right, k_left, pyh in ((own_right, own_left, yhi), (other_right, other_left, yoh)):
        arrived(k_right, rows_of(xo, pyh, half, half))
        arrived(k_left, rows_of(xo, pyh, 0, half))
    source_product(xo)

    parts[...] = jnp.zeros_like(parts)
    r_iota = lax.broadcasted_iota(jnp.int32, (256, 256), 0)
    c_iota = lax.broadcasted_iota(jnp.int32, (256, 256), 1)
    same = lax.rem(r_iota, 16) == lax.rem(c_iota, 16)
    pick_row = lax.broadcasted_iota(jnp.int32, (16, 256), 0)
    pick_group = lax.broadcasted_iota(jnp.int32, (16, 256), 1) // 16
    straight = jnp.where(pick_row == pick_group, 1.0, 0.0)
    crossed = jnp.where(
        pick_row < 8,
        jnp.where(pick_group == pick_row + 8, -1.0, 0.0),
        jnp.where(pick_group == pick_row - 8, 1.0, 0.0),
    )

    def trace(u):
        total = jnp.zeros((256, 256), jnp.float32)
        for s in range(rows // 16):
            a = xs[u, :, :, 16 * s : 16 * s + 16, :].reshape(256, 512)
            b = ys[u, :, :, 16 * s : 16 * s + 16, :].reshape(256, 512)
            total += dot_nt(a, b)
        total = jnp.where(same, total, 0.0)
        rowed = jnp.sum(total.reshape(16, 16, 256), axis=1)
        re_rows = rowed[0:8]
        im_rows = rowed[8:16]
        plain = exact_nt(re_rows, straight) + exact_nt(im_rows, crossed)
        turned = jnp.concatenate([-im_rows, re_rows], axis=0)
        mirror = exact_nt(straight[0:8], rowed) + exact_nt(straight[8:16], turned)
        parts[taus[u], cores[u], 0:8, 0:16] = plain
        parts[taus[u], cores[u], 8:16, 0:16] = mirror

    for u in range(UNITS):
        trace(u)

    part_copies = []
    for step in range(1, 8):
        to = lax.rem(snk + step, 8)
        copy = pltpu.make_async_remote_copy(
            src_ref=parts.at[to], dst_ref=sums.at[step], send_sem=part_send.at[step],
            recv_sem=part_recv.at[step], device_id=(src, to), device_id_type=MESH,
        )
        copy.start()
        part_copies.append(copy)
    sums[0] = parts[snk]
    for copy in part_copies:
        copy.wait()
    sums[0] = jnp.sum(sums[...], axis=0)
    def swap_copy(c):
        return pltpu.make_async_remote_copy(
            src_ref=sums.at[0, c], dst_ref=swapped.at[core], send_sem=swap_send.at[c],
            recv_sem=swap_recv.at[core], device_id=(snk * 2 + c, tau), device_id_type=MESH,
        )

    @pl.when(outside)
    def _():
        for c in range(2):
            swap_copy(c).start()
        for c in range(2):
            swap_copy(c).wait_send()
            pltpu.make_async_remote_copy(
                src_ref=sums.at[0, c], dst_ref=swapped.at[c], send_sem=swap_send.at[c],
                recv_sem=swap_recv.at[c], device_id=(snk * 2 + c, tau), device_id_type=MESH,
            ).wait_recv()

    for c in range(2):
        value = sums[0, c, 0:8, :] + swapped[c, 8:16, :]
        out[0, 0, c] = value[:, 0:8]
        out[1, 0, c] = value[:, 8:16]
    for copy in sent:
        copy.wait_send()
    half_copy(mine).wait_send()


def on_device(perambulators, elements):
    ops, rows, width = elements.shape[1], elements.shape[3], elements.shape[4]
    bf16, f32 = jnp.bfloat16, jnp.float32
    copies = 20
    return pl.pallas_call(
        kernel,
        out_shape=jax.ShapeDtypeStruct((2, 1, 2, ops, ops), f32),
        in_specs=[pl.BlockSpec(memory_space=pl.ANY)] * 2,
        out_specs=pl.BlockSpec(memory_space=pltpu.VMEM),
        scratch_shapes=[
            pltpu.VMEM((ops, 2, width, width), bf16),
            pltpu.VMEM((9, ops, 2, rows, width), bf16),
            pltpu.VMEM((UNITS, 2, width, width), bf16),
            pltpu.VMEM((2, UNITS, 2, rows, width), bf16),
            pltpu.VMEM((UNITS, 2, ops, rows, width), bf16),
            pltpu.VMEM((UNITS, 2, ops, rows, width), bf16),
            pltpu.VMEM((8, 2, 16, 128), f32),
            pltpu.VMEM((8, 2, 16, 128), f32),
            pltpu.VMEM((2, 16, 128), f32),
            pltpu.SemaphoreType.DMA((UNITS + 1,)),
            pltpu.SemaphoreType.DMA((copies,)),
            pltpu.SemaphoreType.DMA((copies,)),
            pltpu.SemaphoreType.DMA((8,)),
            pltpu.SemaphoreType.DMA((8,)),
            pltpu.SemaphoreType.DMA((2,)),
            pltpu.SemaphoreType.DMA((2,)),
        ],
        compiler_params=pltpu.CompilerParams(
            collective_id=0, has_side_effects=True, vmem_limit_bytes=62 * 2**20
        ),
        cost_estimate=pl.CostEstimate(
            flops=20 * 10**9, bytes_accessed=12 * 2**20, transcendentals=0
        ),
        name="correlate",
    )(perambulators, elements)


def solution(mesh):
    placed = (P("src", None, None, None, None), P("src", None, None, "snk", None))
    return jax.shard_map(
        on_device,
        mesh=mesh,
        in_specs=placed,
        out_specs=P(None, "src", "snk", None, None),
        check_vma=False,
    )
```

```python
import jax
import jax.numpy as jnp
from jax import lax
from jax.experimental import pallas as pl
from jax.experimental.pallas import tpu as pltpu
from jax.sharding import PartitionSpec as P

MESH = pl.DeviceIdType.MESH
UNITS = 9
NT_DIMS = (((1,), (1,)), ((), ()))

FLIP, NEXT, FLIP_PREV, HALF = 0, 1, 2, 3
SIB_OWN, SIB_FLIP, SIB_NEXT, SIB_FLIP_PREV, SIB_HALF = 4, 5, 6, 7, 8


def dot(a, b):
    return jnp.dot(a, b, preferred_element_type=jnp.float32)


def dot_nt(a, b):
    return lax.dot_general(a, b, NT_DIMS, preferred_element_type=jnp.float32)


def exact_nt(a, b):
    return lax.dot_general(
        a, b, NT_DIMS, preferred_element_type=jnp.float32, precision=lax.Precision.HIGHEST
    )


def kernel(
    peram, elem, out, full, other, mats, left, xs, ys, gram, rowed, parts, sums, swapped,
    load_sem, send_sem, recv_sem, part_send, part_recv, swap_send, swap_recv,
):
    src = lax.axis_index("src")
    snk = lax.axis_index("snk")
    core = lax.rem(src, 2)
    z = lax.rem(src // 2, 4)
    ylo = src // 8
    x = snk // 2
    yhi = lax.rem(snk, 2)
    y = yhi * 2 + ylo
    tau = src // 2
    ops = elem.shape[1]
    rows = elem.shape[3]

    def place(px, py, pz, pc):
        return ((lax.rem(py, 2) * 4 + pz) * 2 + pc, px * 2 + py // 2)

    xr = lax.rem(x + 1, 4)
    xl = lax.rem(x + 3, 4)
    xo = lax.rem(x + 2, 4)
    yn = lax.rem(y + 1, 4)
    yp = lax.rem(y + 3, 4)
    yo = lax.rem(y + 2, 4)
    zn = lax.rem(z + 1, 4)
    zp = lax.rem(z + 3, 4)
    zo = lax.rem(z + 2, 4)
    yoh = yo // 2
    dev_xr = place(xr, y, z, core)
    dev_xl = place(xl, y, z, core)
    dev_yo = place(x, yo, z, core)
    y_to = lax.rem(y + 3 + 2 * core, 4)
    y_from = lax.rem(y + 1 + 2 * core, 4)
    y_from_sib = lax.rem(y + 3 + 2 * core, 4)
    dev_flip = place(x, y_to, z, core)
    dev_flip_back = place(x, y_from, z, core)
    dev_zn = place(x, y, zn, core)
    dev_zp = place(x, y, zp, core)
    dev_zo = place(x, y, zo, core)
    dev_sib = (src + 1 - 2 * core, snk)

    own_rows = snk
    flip_rows = x * 2 + y_from // 2
    flip_rows_sib = x * 2 + y_from_sib // 2
    low = z < 2
    flip_tau = (1 - ylo) * 4 + z
    next_tau = ylo * 4 + zn
    prev_tau = (1 - ylo) * 4 + zp
    half_tau = jnp.where(low, ylo, 1 - ylo) * 4 + zo
    sib = 1 - core
    flip_core = lax.rem(core + ylo, 2)
    taus = [tau, tau, flip_tau, next_tau, next_tau, prev_tau, prev_tau, half_tau, half_tau]
    cores = [core, sib, flip_core, core, sib, core, sib, core, sib]
    blocks = [
        own_rows,
        own_rows,
        jnp.where(ylo == 0, flip_rows, flip_rows_sib),
        own_rows,
        own_rows,
        flip_rows,
        flip_rows_sib,
        jnp.where(low, own_rows, flip_rows),
        jnp.where(low, own_rows, flip_rows_sib),
    ]
    slots = [
        None, SIB_OWN, jnp.where(ylo == 0, FLIP, SIB_FLIP), NEXT, SIB_NEXT,
        FLIP_PREV, SIB_FLIP_PREV, HALF, SIB_HALF,
    ]

    own_slice = full.at[:, :, pl.ds(pl.multiple_of(snk * rows, rows), rows), :]
    own_load = pltpu.make_async_copy(elem.at[0], own_slice, load_sem.at[UNITS])
    own_load.start()
    loads = []
    for u in range(UNITS):
        load = pltpu.make_async_copy(
            peram.at[0, taus[u] * 2 + cores[u]], mats.at[u], load_sem.at[u]
        )
        load.start()
        loads.append(load)

    swapped[...] = jnp.zeros_like(swapped)

    barrier = pltpu.get_barrier_semaphore()
    for step in range(1, 8):
        pl.semaphore_signal(
            barrier, inc=1, device_id=(src, lax.rem(snk + step, 8)), device_id_type=MESH
        )
    for target in (dev_flip, dev_flip_back, dev_zn, dev_zp, dev_zo, dev_sib):
        pl.semaphore_signal(barrier, inc=1, device_id=target, device_id_type=MESH)
    outside = snk != tau

    @pl.when(outside)
    def _():
        for c in range(2):
            pl.semaphore_signal(barrier, inc=1, device_id=(snk * 2 + c, tau), device_id_type=MESH)

    pl.semaphore_wait(barrier, jnp.where(outside, 15, 13))

    sent = []
    counter = [0]

    def remote(source, target, device):
        k = counter[0]
        counter[0] += 1
        copy = pltpu.make_async_remote_copy(
            src_ref=source, dst_ref=target, send_sem=send_sem.at[k], recv_sem=recv_sem.at[k],
            device_id=device, device_id_type=MESH,
        )
        copy.start()
        sent.append(copy)
        return k

    def arrived(k, target):
        pltpu.make_async_remote_copy(
            src_ref=target, dst_ref=target, send_sem=send_sem.at[k], recv_sem=recv_sem.at[k],
            device_id=dev_sib, device_id_type=MESH,
        ).wait_recv()

    def rows_of(px, pyh, first=0, count=ops):
        start = pl.multiple_of((px * 2 + pyh) * rows, rows)
        return full.at[pl.ds(first, count), :, pl.ds(start, rows), :]

    half = ops // 2
    lower, upper = (0, half), (half, half)

    def cut(ref, piece):
        return ref.at[pl.ds(*piece)]

    mine = elem.at[0]
    k_half = counter[0]
    counter[0] += 1

    def half_copy(source):
        return pltpu.make_async_remote_copy(
            src_ref=source, dst_ref=other.at[HALF], send_sem=send_sem.at[k_half],
            recv_sem=recv_sem.at[k_half], device_id=dev_zo, device_id_type=MESH,
        )

    def to_both_sides(source, pyh):
        sends = {}
        for piece, device in (
            (upper, dev_xr), (lower, dev_xl), (lower, dev_xr), (upper, dev_xl)
        ):
            sends[piece, device is dev_xr] = remote(
                cut(source, piece), rows_of(x, pyh, *piece), device
            )
        return sends

    def pass_on(sends, pyh):
        arrived(sends[upper, True], rows_of(xl, pyh, *upper))
        on_right = remote(rows_of(xl, pyh, *upper), rows_of(xl, pyh, *upper), dev_xr)
        arrived(sends[lower, False], rows_of(xr, pyh, *lower))
        on_left = remote(rows_of(xr, pyh, *lower), rows_of(xr, pyh, *lower), dev_xl)
        return on_right, on_left

    def rest_arrived(sends, pyh):
        arrived(sends[lower, True], rows_of(xl, pyh, *lower))
        arrived(sends[upper, False], rows_of(xr, pyh, *upper))

    def passed_arrived(ks, pyh):
        arrived(ks[0], rows_of(xo, pyh, *upper))
        arrived(ks[1], rows_of(xo, pyh, *lower))

    k_flip = [
        remote(cut(mine, piece), cut(other.at[FLIP], piece), dev_flip) for piece in (lower, upper)
    ]
    own_sends = to_both_sides(mine, yhi)
    k_next = remote(mine, other.at[NEXT], dev_zp)

    @pl.when(jnp.logical_not(low))
    def _():
        half_copy(mine).start()

    k_sib = remote(mine, other.at[SIB_OWN], dev_sib)

    col = lax.broadcasted_iota(jnp.int32, (rows, 512), 1)
    lane_sign = jnp.where(col < 256, 1.0, -1.0) * jnp.where(x < 2, 1.0, -1.0)

    def prepare(u):
        loads[u].wait()
        start = pl.multiple_of(blocks[u] * rows, rows)
        re = mats[u, 0, pl.ds(start, rows), :].astype(jnp.float32) * lane_sign
        im = mats[u, 1, pl.ds(start, rows), :].astype(jnp.float32) * lane_sign
        left[0, u, 0] = re.astype(jnp.bfloat16)
        left[0, u, 1] = (-im).astype(jnp.bfloat16)
        left[1, u, 0] = im.astype(jnp.bfloat16)
        left[1, u, 1] = re.astype(jnp.bfloat16)

    def sink_product(u):
        def tile(n, carry):
            cols = pl.ds(pl.multiple_of(n * 256, 256), 256)
            if u == 0:
                start = pl.multiple_of(snk * rows, rows)
                er = full[:, 0, pl.ds(start, rows), :]
                ei = full[:, 1, pl.ds(start, rows), :]
            else:
                er = other[slots[u], :, 0]
                ei = other[slots[u], :, 1]
            er = er.reshape(ops * rows, 512)
            ei = ei.reshape(ops * rows, 512)
            pr = mats[u, 0, :, cols]
            pi = mats[u, 1, :, cols]
            re = dot(er, pr) - dot(ei, pi)
            im = dot(er, pi) + dot(ei, pr)
            xs[u, 0, :, :, cols] = re.astype(jnp.bfloat16).reshape(ops, rows, 256)
            xs[u, 1, :, :, cols] = im.astype(jnp.bfloat16).reshape(ops, rows, 256)
            return carry

        lax.fori_loop(0, 2, tile, 0)

    lane = lax.broadcasted_iota(jnp.int32, (384, 128), 1)

    def source_product(px, pyh, first):
        cols = pl.ds(pl.multiple_of(px * 128, 128), 128)
        krows = pl.ds(pl.multiple_of((px * 2 + pyh) * rows, rows), rows)
        here = (lane // 64) == pyh

        def tile(q, carry):
            wr = full[pl.ds(q * 4, 4), 0, krows, :].reshape(256, 512)
            wi = full[pl.ds(q * 4, 4), 1, krows, :].reshape(256, 512)
            for m in range(3):
                units = slice(3 * m, 3 * m + 3)
                a = left[0, units].reshape(384, 512)
                b = left[1, units].reshape(384, 512)
                r = dot_nt(a, wr) + dot_nt(b, wi)
                for j in range(2):
                    v = r[:, 128 * j : 128 * j + 128]
                    w = pltpu.roll(v, 64, 1)
                    for k, new in enumerate(
                        (jnp.where(lane < 64, v, w), jnp.where(lane < 64, w, v))
                    ):
                        o = q * 4 + 2 * j + k
                        if not first:
                            old = ys[units, :, o, :, cols].reshape(384, 128)
                            new = jnp.where(here, new, old.astype(jnp.float32))
                        ys[units, :, o, :, cols] = new.astype(jnp.bfloat16).reshape(
                            3, 2, rows, 128
                        )
            return carry

        lax.fori_loop(0, 2, tile, 0)

    r_iota = lax.broadcasted_iota(jnp.int32, (256, 256), 0)
    c_iota = lax.broadcasted_iota(jnp.int32, (256, 256), 1)
    same = lax.rem(r_iota, 16) == lax.rem(c_iota, 16)

    def trace(columns, last):
        def unit(u, carry):
            total = None
            for s in range(rows // 16):
                picked = []
                for held in (xs, ys):
                    picked.append(jnp.concatenate(
                        [
                            held[u, :, :, 16 * s : 16 * s + 16,
                                 pl.ds(pl.multiple_of(px * 128, 128), 128)].reshape(256, 128)
                            for px in columns
                        ],
                        axis=1,
                    ))
                product = dot_nt(*picked)
                total = product if total is None else total + product
            if last:
                total = jnp.where(same, total + gram[u], 0.0)
                rowed[u] = jnp.sum(total.reshape(2 * ops, 16, 256), axis=1)
            else:
                gram[u] = total
            return carry

        lax.fori_loop(0, UNITS, unit, 0)

    own_load.wait()
    for u in range(UNITS):
        prepare(u)
    sink_product(0)
    k_yo, k_prev = [], []

    def relay(i, piece):
        arrived(k_flip[i], cut(other.at[FLIP], piece))
        k_yo.append(
            remote(cut(other.at[FLIP], piece), rows_of(x, y_from // 2, *piece), dev_flip)
        )
        k_prev.append(
            remote(cut(other.at[FLIP], piece), cut(other.at[FLIP_PREV], piece), dev_zn)
        )

    relay(0, lower)
    source_product(x, yhi, True)
    relay(1, upper)

    @pl.when(low)
    def _():
        half_copy(other.at[FLIP]).start()

    k_sib_flip = remote(other.at[FLIP], other.at[SIB_FLIP], dev_sib)
    arrived(k_sib, other.at[SIB_OWN])
    sink_product(1)
    own_passed = pass_on(own_sends, yhi)
    arrived(k_sib_flip, other.at[SIB_FLIP])
    sink_product(2)
    arrived(k_yo[0], rows_of(x, yoh, *lower))
    arrived(k_yo[1], rows_of(x, yoh, *upper))
    other_sends = to_both_sides(rows_of(x, yoh), yoh)
    source_product(x, yoh, False)
    rest_arrived(own_sends, yhi)
    source_product(xl, yhi, True)
    source_product(xr, yhi, True)
    arrived(k_next, other.at[NEXT])
    k_sib_next = remote(other.at[NEXT], other.at[SIB_NEXT], dev_sib)
    sink_product(3)
    arrived(k_sib_next, other.at[SIB_NEXT])
    sink_product(4)
    passed_arrived(own_passed, yhi)
    source_product(xo, yhi, True)
    arrived(k_prev[0], cut(other.at[FLIP_PREV], lower))
    arrived(k_prev[1], cut(other.at[FLIP_PREV], upper))
    k_sib_prev = remote(other.at[FLIP_PREV], other.at[SIB_FLIP_PREV], dev_sib)
    sink_product(5)
    arrived(k_sib_prev, other.at[SIB_FLIP_PREV])
    sink_product(6)
    other_passed = pass_on(other_sends, yoh)
    arrived(k_half, other.at[HALF])
    k_sib_half = remote(other.at[HALF], other.at[SIB_HALF], dev_sib)
    sink_product(7)
    arrived(k_sib_half, other.at[SIB_HALF])
    sink_product(8)
    rest_arrived(other_sends, yoh)
    source_product(xl, yoh, False)
    source_product(xr, yoh, False)
    trace((x, xl, xr), False)
    passed_arrived(other_passed, yoh)
    source_product(xo, yoh, False)
    trace((xo,), True)

    parts[...] = jnp.zeros_like(parts)
    pick_row = lax.broadcasted_iota(jnp.int32, (16, 256), 0)
    pick_group = lax.broadcasted_iota(jnp.int32, (16, 256), 1) // 16
    straight = jnp.where(pick_row == pick_group, 1.0, 0.0)
    crossed = jnp.where(
        pick_row < 8,
        jnp.where(pick_group == pick_row + 8, -1.0, 0.0),
        jnp.where(pick_group == pick_row - 8, 1.0, 0.0),
    )
    traces = exact_nt(rowed[:, 0:8].reshape(UNITS * 8, 256), straight) + exact_nt(
        rowed[:, 8:16].reshape(UNITS * 8, 256), crossed
    )
    for u in range(UNITS):
        parts[taus[u], cores[u], :, 0:16] = traces[8 * u : 8 * u + 8]

    part_copies = []
    for step in range(1, 8):
        to = lax.rem(snk + step, 8)
        copy = pltpu.make_async_remote_copy(
            src_ref=parts.at[to], dst_ref=sums.at[step], send_sem=part_send.at[step],
            recv_sem=part_recv.at[step], device_id=(src, to), device_id_type=MESH,
        )
        copy.start()
        part_copies.append(copy)
    sums[0] = parts[snk]
    for copy in part_copies:
        copy.wait()
    sums[0] = jnp.sum(sums[...], axis=0)
    def swap_copy(c):
        return pltpu.make_async_remote_copy(
            src_ref=sums.at[0, c], dst_ref=swapped.at[core], send_sem=swap_send.at[c],
            recv_sem=swap_recv.at[core], device_id=(snk * 2 + c, tau), device_id_type=MESH,
        )

    @pl.when(outside)
    def _():
        for c in range(2):
            swap_copy(c).start()
        for c in range(2):
            swap_copy(c).wait_send()
            pltpu.make_async_remote_copy(
                src_ref=sums.at[0, c], dst_ref=swapped.at[c], send_sem=swap_send.at[c],
                recv_sem=swap_recv.at[c], device_id=(snk * 2 + c, tau), device_id_type=MESH,
            ).wait_recv()

    turn_row = lax.broadcasted_iota(jnp.int32, (8, 128), 0)
    turn_lane = lax.broadcasted_iota(jnp.int32, (8, 128), 1)
    for c in range(2):
        for part in range(2):
            turn = jnp.where(turn_lane == turn_row + 8 * part, 1.0, 0.0)
            out[part, 0, c] = sums[0, c, :, 8 * part : 8 * part + 8] + exact_nt(turn, swapped[c])
    for copy in sent:
        copy.wait_send()
    half_copy(mine).wait_send()


def on_device(perambulators, elements):
    ops, rows, width = elements.shape[1], elements.shape[3], elements.shape[4]
    bf16, f32 = jnp.bfloat16, jnp.float32
    copies = 32
    return pl.pallas_call(
        kernel,
        out_shape=jax.ShapeDtypeStruct((2, 1, 2, ops, ops), f32),
        in_specs=[pl.BlockSpec(memory_space=pl.ANY)] * 2,
        out_specs=pl.BlockSpec(memory_space=pltpu.VMEM),
        scratch_shapes=[
            pltpu.VMEM((ops, 2, width, width), bf16),
            pltpu.VMEM((9, ops, 2, rows, width), bf16),
            pltpu.VMEM((UNITS, 2, width, width), bf16),
            pltpu.VMEM((2, UNITS, 2, rows, width), bf16),
            pltpu.VMEM((UNITS, 2, ops, rows, width), bf16),
            pltpu.VMEM((UNITS, 2, ops, rows, width), bf16),
            pltpu.VMEM((UNITS, 256, 256), f32),
            pltpu.VMEM((UNITS, 16, 256), f32),
            pltpu.VMEM((8, 2, 8, 128), f32),
            pltpu.VMEM((8, 2, 8, 128), f32),
            pltpu.VMEM((2, 8, 128), f32),
            pltpu.SemaphoreType.DMA((UNITS + 1,)),
            pltpu.SemaphoreType.DMA((copies,)),
            pltpu.SemaphoreType.DMA((copies,)),
            pltpu.SemaphoreType.DMA((8,)),
            pltpu.SemaphoreType.DMA((8,)),
            pltpu.SemaphoreType.DMA((2,)),
            pltpu.SemaphoreType.DMA((2,)),
        ],
        compiler_params=pltpu.CompilerParams(
            collective_id=0, has_side_effects=True, vmem_limit_bytes=62 * 2**20
        ),
        cost_estimate=pl.CostEstimate(
            flops=20 * 10**9, bytes_accessed=12 * 2**20, transcendentals=0
        ),
        name="correlate",
    )(perambulators, elements)


def solution(mesh):
    placed = (P("src", None, None, None, None), P("src", None, None, "snk", None))
    return jax.shard_map(
        on_device,
        mesh=mesh,
        in_specs=placed,
        out_specs=P(None, "src", "snk", None, None),
        check_vma=False,
    )
```

```python
import jax
import jax.numpy as jnp
from jax import lax
from jax.experimental import pallas as pl
from jax.experimental.pallas import tpu as pltpu
from jax.sharding import PartitionSpec as P

MESH = pl.DeviceIdType.MESH
UNITS = 9
NT_DIMS = (((1,), (1,)), ((), ()))

FLIP, NEXT, FLIP_PREV, HALF = 0, 1, 2, 3
SIB_OWN, SIB_FLIP, SIB_NEXT, SIB_FLIP_PREV, SIB_HALF = 4, 5, 6, 7, 8


def dot(a, b):
    return jnp.dot(a, b, preferred_element_type=jnp.float32)


def dot_nt(a, b):
    return lax.dot_general(a, b, NT_DIMS, preferred_element_type=jnp.float32)


def exact_nt(a, b):
    return lax.dot_general(
        a, b, NT_DIMS, preferred_element_type=jnp.float32, precision=lax.Precision.HIGHEST
    )


def kernel(
    peram, elem, out, full, other, mats, left, xs, ys, gram, rowed, parts, sums, swapped,
    load_sem, send_sem, recv_sem, part_send, part_recv, swap_send, swap_recv,
):
    src = lax.axis_index("src")
    snk = lax.axis_index("snk")
    core = lax.rem(src, 2)
    z = lax.rem(src // 2, 4)
    ylo = src // 8
    x = snk // 2
    yhi = lax.rem(snk, 2)
    y = yhi * 2 + ylo
    tau = src // 2
    ops = elem.shape[1]
    rows = elem.shape[3]

    def place(px, py, pz, pc):
        return ((lax.rem(py, 2) * 4 + pz) * 2 + pc, px * 2 + py // 2)

    xf = lax.rem(x + 1 + 2 * core, 4)
    xb = lax.rem(x + 3 + 2 * core, 4)
    xo = lax.rem(x + 2, 4)
    yn = lax.rem(y + 1, 4)
    yp = lax.rem(y + 3, 4)
    yo = lax.rem(y + 2, 4)
    zn = lax.rem(z + 1, 4)
    zp = lax.rem(z + 3, 4)
    zo = lax.rem(z + 2, 4)
    yoh = yo // 2
    dev_fore = place(xf, y, z, core)
    dev_back = place(xb, y, z, core)
    dev_yo = place(x, yo, z, core)
    y_to = lax.rem(y + 3 + 2 * core, 4)
    y_from = lax.rem(y + 1 + 2 * core, 4)
    y_from_sib = lax.rem(y + 3 + 2 * core, 4)
    dev_flip = place(x, y_to, z, core)
    dev_flip_back = place(x, y_from, z, core)
    dev_zn = place(x, y, zn, core)
    dev_zp = place(x, y, zp, core)
    dev_zo = place(x, y, zo, core)
    dev_sib = (src + 1 - 2 * core, snk)

    own_rows = snk
    flip_rows = x * 2 + y_from // 2
    flip_rows_sib = x * 2 + y_from_sib // 2
    low = z < 2
    flip_tau = (1 - ylo) * 4 + z
    next_tau = ylo * 4 + zn
    prev_tau = (1 - ylo) * 4 + zp
    half_tau = jnp.where(low, ylo, 1 - ylo) * 4 + zo
    sib = 1 - core
    flip_core = lax.rem(core + ylo, 2)
    taus = [tau, tau, flip_tau, next_tau, next_tau, prev_tau, prev_tau, half_tau, half_tau]
    cores = [core, sib, flip_core, core, sib, core, sib, core, sib]
    blocks = [
        own_rows,
        own_rows,
        jnp.where(ylo == 0, flip_rows, flip_rows_sib),
        own_rows,
        own_rows,
        flip_rows,
        flip_rows_sib,
        jnp.where(low, own_rows, flip_rows),
        jnp.where(low, own_rows, flip_rows_sib),
    ]
    slots = [
        None, SIB_OWN, jnp.where(ylo == 0, FLIP, SIB_FLIP), NEXT, SIB_NEXT,
        FLIP_PREV, SIB_FLIP_PREV, HALF, SIB_HALF,
    ]

    own_slice = full.at[:, :, pl.ds(pl.multiple_of(snk * rows, rows), rows), :]
    own_load = pltpu.make_async_copy(elem.at[0], own_slice, load_sem.at[UNITS])
    own_load.start()
    loads = []
    for u in range(UNITS):
        load = pltpu.make_async_copy(
            peram.at[0, taus[u] * 2 + cores[u]], mats.at[u], load_sem.at[u]
        )
        load.start()
        loads.append(load)

    swapped[...] = jnp.zeros_like(swapped)

    barrier = pltpu.get_barrier_semaphore()
    for step in range(1, 8):
        pl.semaphore_signal(
            barrier, inc=1, device_id=(src, lax.rem(snk + step, 8)), device_id_type=MESH
        )
    for target in (dev_flip, dev_flip_back, dev_zn, dev_zp, dev_zo, dev_sib):
        pl.semaphore_signal(barrier, inc=1, device_id=target, device_id_type=MESH)
    outside = snk != tau

    @pl.when(outside)
    def _():
        for c in range(2):
            pl.semaphore_signal(barrier, inc=1, device_id=(snk * 2 + c, tau), device_id_type=MESH)

    pl.semaphore_wait(barrier, jnp.where(outside, 15, 13))

    sent = []
    counter = [0]

    def remote(source, target, device):
        k = counter[0]
        counter[0] += 1
        copy = pltpu.make_async_remote_copy(
            src_ref=source, dst_ref=target, send_sem=send_sem.at[k], recv_sem=recv_sem.at[k],
            device_id=device, device_id_type=MESH,
        )
        copy.start()
        sent.append(copy)
        return k

    def arrived(k, target):
        pltpu.make_async_remote_copy(
            src_ref=target, dst_ref=target, send_sem=send_sem.at[k], recv_sem=recv_sem.at[k],
            device_id=dev_sib, device_id_type=MESH,
        ).wait_recv()

    def rows_of(px, pyh, first=0, count=ops):
        start = pl.multiple_of((px * 2 + pyh) * rows, rows)
        return full.at[pl.ds(first, count), :, pl.ds(start, rows), :]

    quarters = ((0, 2), (2, 2), (4, 2), (6, 2))
    tail, fifth, head = (5, 3), (4, 1), (0, 4)
    pair, triple = (0, 2), (2, 3)

    def cut(ref, piece):
        return ref.at[pl.ds(*piece)]

    mine = elem.at[0]
    k_half = counter[0]
    counter[0] += 1

    def half_copy(source):
        return pltpu.make_async_remote_copy(
            src_ref=source, dst_ref=other.at[HALF], send_sem=send_sem.at[k_half],
            recv_sem=recv_sem.at[k_half], device_id=dev_zo, device_id_type=MESH,
        )

    def block(px, pyh, piece):
        return rows_of(px, pyh, *piece)

    k_flip = [remote(cut(mine, q), cut(other.at[FLIP], q), dev_flip) for q in quarters]
    k_own_fore, k_own_back = {}, {}
    for piece in (tail, fifth, head):
        k_own_fore[piece] = remote(cut(mine, piece), block(x, yhi, piece), dev_fore)
        k_own_back[piece] = remote(cut(mine, piece), block(x, yhi, piece), dev_back)
    k_next = remote(mine, other.at[NEXT], dev_zp)

    @pl.when(jnp.logical_not(low))
    def _():
        half_copy(mine).start()

    k_sib = remote(mine, other.at[SIB_OWN], dev_sib)

    col = lax.broadcasted_iota(jnp.int32, (rows, 512), 1)
    lane_sign = jnp.where(col < 256, 1.0, -1.0) * jnp.where(x < 2, 1.0, -1.0)

    def prepare(u):
        loads[u].wait()
        start = pl.multiple_of(blocks[u] * rows, rows)
        re = mats[u, 0, pl.ds(start, rows), :].astype(jnp.float32) * lane_sign
        im = mats[u, 1, pl.ds(start, rows), :].astype(jnp.float32) * lane_sign
        left[0, u, 0] = re.astype(jnp.bfloat16)
        left[0, u, 1] = (-im).astype(jnp.bfloat16)
        left[1, u, 0] = im.astype(jnp.bfloat16)
        left[1, u, 1] = re.astype(jnp.bfloat16)

    def sink_product(u):
        def tile(n, carry):
            cols = pl.ds(pl.multiple_of(n * 256, 256), 256)
            if u == 0:
                start = pl.multiple_of(snk * rows, rows)
                er = full[:, 0, pl.ds(start, rows), :]
                ei = full[:, 1, pl.ds(start, rows), :]
            else:
                er = other[slots[u], :, 0]
                ei = other[slots[u], :, 1]
            er = er.reshape(ops * rows, 512)
            ei = ei.reshape(ops * rows, 512)
            pr = mats[u, 0, :, cols]
            pi = mats[u, 1, :, cols]
            re = dot(er, pr) - dot(ei, pi)
            im = dot(er, pi) + dot(ei, pr)
            xs[u, 0, :, :, cols] = re.astype(jnp.bfloat16).reshape(ops, rows, 256)
            xs[u, 1, :, :, cols] = im.astype(jnp.bfloat16).reshape(ops, rows, 256)
            return carry

        lax.fori_loop(0, 2, tile, 0)

    lane = lax.broadcasted_iota(jnp.int32, (384, 128), 1)

    def source_product(px, pyh, first):
        cols = pl.ds(pl.multiple_of(px * 128, 128), 128)
        krows = pl.ds(pl.multiple_of((px * 2 + pyh) * rows, rows), rows)
        here = (lane // 64) == pyh

        def tile(q, carry):
            wr = full[pl.ds(q * 4, 4), 0, krows, :].reshape(256, 512)
            wi = full[pl.ds(q * 4, 4), 1, krows, :].reshape(256, 512)
            for m in range(3):
                units = slice(3 * m, 3 * m + 3)
                a = left[0, units].reshape(384, 512)
                b = left[1, units].reshape(384, 512)
                r = dot_nt(a, wr) + dot_nt(b, wi)
                for j in range(2):
                    v = r[:, 128 * j : 128 * j + 128]
                    w = pltpu.roll(v, 64, 1)
                    for k, new in enumerate(
                        (jnp.where(lane < 64, v, w), jnp.where(lane < 64, w, v))
                    ):
                        o = q * 4 + 2 * j + k
                        if not first:
                            old = ys[units, :, o, :, cols].reshape(384, 128)
                            new = jnp.where(here, new, old.astype(jnp.float32))
                        ys[units, :, o, :, cols] = new.astype(jnp.bfloat16).reshape(
                            3, 2, rows, 128
                        )
            return carry

        lax.fori_loop(0, 2, tile, 0)

    r_iota = lax.broadcasted_iota(jnp.int32, (256, 256), 0)
    c_iota = lax.broadcasted_iota(jnp.int32, (256, 256), 1)
    same = lax.rem(r_iota, 16) == lax.rem(c_iota, 16)

    def trace(columns, last):
        def unit(u, carry):
            total = None
            for s in range(rows // 16):
                picked = []
                for held in (xs, ys):
                    picked.append(jnp.concatenate(
                        [
                            held[u, :, :, 16 * s : 16 * s + 16,
                                 pl.ds(pl.multiple_of(px * 128, 128), 128)].reshape(256, 128)
                            for px in columns
                        ],
                        axis=1,
                    ))
                product = dot_nt(*picked)
                total = product if total is None else total + product
            if last:
                total = jnp.where(same, total + gram[u], 0.0)
                rowed[u] = jnp.sum(total.reshape(2 * ops, 16, 256), axis=1)
            else:
                gram[u] = total
            return carry

        lax.fori_loop(0, UNITS, unit, 0)

    own_load.wait()
    for u in range(UNITS):
        prepare(u)
    sink_product(0)
    k_yo, k_prev = [], []

    def relay(i):
        q = quarters[i]
        arrived(k_flip[i], cut(other.at[FLIP], q))
        k_yo.append(remote(cut(other.at[FLIP], q), block(x, y_from // 2, q), dev_flip))
        k_prev.append(remote(cut(other.at[FLIP], q), cut(other.at[FLIP_PREV], q), dev_zn))

    def partner(i):
        arrived(k_yo[i], block(x, yoh, quarters[i]))

    def partner_send(piece):
        mine_too = block(x, yoh, piece)
        if piece is pair:
            k_part_fore[piece] = remote(mine_too, mine_too, dev_fore)
            k_part_back[piece] = remote(mine_too, mine_too, dev_back)
        else:
            k_part_back[piece] = remote(mine_too, mine_too, dev_back)
            k_part_fore[piece] = remote(mine_too, mine_too, dev_fore)

    relay(0)
    relay(1)
    source_product(x, yhi, True)
    relay(2)
    relay(3)

    @pl.when(low)
    def _():
        half_copy(other.at[FLIP]).start()

    k_sib_flip = remote(other.at[FLIP], other.at[SIB_FLIP], dev_sib)
    arrived(k_own_fore[tail], block(xb, yhi, tail))
    k_pass_tail = remote(block(xb, yhi, tail), block(xb, yhi, tail), dev_fore)
    k_cross_b = remote(block(xb, yhi, tail), block(xb, yhi, tail), dev_yo)
    arrived(k_own_back[tail], block(xf, yhi, tail))
    k_cross_f = remote(block(xf, yhi, tail), block(xf, yhi, tail), dev_yo)
    arrived(k_sib, other.at[SIB_OWN])
    sink_product(1)
    arrived(k_sib_flip, other.at[SIB_FLIP])
    sink_product(2)
    k_part_fore, k_part_back = {}, {}
    partner(0)
    partner_send(pair)
    partner(1)
    partner(2)
    partner_send(triple)
    arrived(k_own_fore[fifth], block(xb, yhi, fifth))
    k_pass_fifth = remote(block(xb, yhi, fifth), block(xb, yhi, fifth), dev_fore)
    arrived(k_own_back[head], block(xf, yhi, head))
    k_pass_head = remote(block(xf, yhi, head), block(xf, yhi, head), dev_back)
    partner(3)
    source_product(x, yoh, False)
    arrived(k_own_fore[head], block(xb, yhi, head))
    source_product(xb, yhi, True)
    arrived(k_pass_tail, block(xo, yhi, tail))
    k_cross_o = remote(block(xo, yhi, tail), block(xo, yhi, tail), dev_yo)
    arrived(k_own_back[fifth], block(xf, yhi, fifth))
    source_product(xf, yhi, True)
    arrived(k_next, other.at[NEXT])
    k_sib_next = remote(other.at[NEXT], other.at[SIB_NEXT], dev_sib)
    sink_product(3)
    arrived(k_sib_next, other.at[SIB_NEXT])
    sink_product(4)
    for i, q in enumerate(quarters):
        arrived(k_prev[i], cut(other.at[FLIP_PREV], q))
    k_sib_prev = remote(other.at[FLIP_PREV], other.at[SIB_FLIP_PREV], dev_sib)
    sink_product(5)
    arrived(k_part_fore[pair], block(xb, yoh, pair))
    k_pass_pair = remote(block(xb, yoh, pair), block(xb, yoh, pair), dev_fore)
    arrived(k_sib_prev, other.at[SIB_FLIP_PREV])
    sink_product(6)
    arrived(k_part_back[triple], block(xf, yoh, triple))
    k_pass_triple = remote(block(xf, yoh, triple), block(xf, yoh, triple), dev_back)
    arrived(k_pass_fifth, block(xo, yhi, fifth))
    arrived(k_pass_head, block(xo, yhi, head))
    source_product(xo, yhi, True)
    arrived(k_half, other.at[HALF])
    k_sib_half = remote(other.at[HALF], other.at[SIB_HALF], dev_sib)
    sink_product(7)
    arrived(k_sib_half, other.at[SIB_HALF])
    sink_product(8)
    arrived(k_part_fore[triple], block(xb, yoh, triple))
    arrived(k_cross_b, block(xb, yoh, tail))
    source_product(xb, yoh, False)
    arrived(k_part_back[pair], block(xf, yoh, pair))
    arrived(k_cross_f, block(xf, yoh, tail))
    source_product(xf, yoh, False)
    trace((x, xf, xb), False)
    arrived(k_cross_o, block(xo, yoh, tail))
    arrived(k_pass_pair, block(xo, yoh, pair))
    arrived(k_pass_triple, block(xo, yoh, triple))
    source_product(xo, yoh, False)
    trace((xo,), True)

    parts[...] = jnp.zeros_like(parts)
    pick_row = lax.broadcasted_iota(jnp.int32, (16, 256), 0)
    pick_group = lax.broadcasted_iota(jnp.int32, (16, 256), 1) // 16
    straight = jnp.where(pick_row == pick_group, 1.0, 0.0)
    crossed = jnp.where(
        pick_row < 8,
        jnp.where(pick_group == pick_row + 8, -1.0, 0.0),
        jnp.where(pick_group == pick_row - 8, 1.0, 0.0),
    )
    traces = exact_nt(rowed[:, 0:8].reshape(UNITS * 8, 256), straight) + exact_nt(
        rowed[:, 8:16].reshape(UNITS * 8, 256), crossed
    )
    for u in range(UNITS):
        parts[taus[u], cores[u], :, 0:16] = traces[8 * u : 8 * u + 8]

    part_copies = []
    for step in range(1, 8):
        to = lax.rem(snk + step, 8)
        copy = pltpu.make_async_remote_copy(
            src_ref=parts.at[to], dst_ref=sums.at[step], send_sem=part_send.at[step],
            recv_sem=part_recv.at[step], device_id=(src, to), device_id_type=MESH,
        )
        copy.start()
        part_copies.append(copy)
    sums[0] = parts[snk]
    for copy in part_copies:
        copy.wait()
    sums[0] = jnp.sum(sums[...], axis=0)
    def swap_copy(c):
        return pltpu.make_async_remote_copy(
            src_ref=sums.at[0, c], dst_ref=swapped.at[core], send_sem=swap_send.at[c],
            recv_sem=swap_recv.at[core], device_id=(snk * 2 + c, tau), device_id_type=MESH,
        )

    @pl.when(outside)
    def _():
        for c in range(2):
            swap_copy(c).start()
        for c in range(2):
            swap_copy(c).wait_send()
            pltpu.make_async_remote_copy(
                src_ref=sums.at[0, c], dst_ref=swapped.at[c], send_sem=swap_send.at[c],
                recv_sem=swap_recv.at[c], device_id=(snk * 2 + c, tau), device_id_type=MESH,
            ).wait_recv()

    turn_row = lax.broadcasted_iota(jnp.int32, (8, 128), 0)
    turn_lane = lax.broadcasted_iota(jnp.int32, (8, 128), 1)
    for c in range(2):
        for part in range(2):
            turn = jnp.where(turn_lane == turn_row + 8 * part, 1.0, 0.0)
            out[part, 0, c] = sums[0, c, :, 8 * part : 8 * part + 8] + exact_nt(turn, swapped[c])
    for copy in sent:
        copy.wait_send()
    half_copy(mine).wait_send()


def on_device(perambulators, elements):
    ops, rows, width = elements.shape[1], elements.shape[3], elements.shape[4]
    bf16, f32 = jnp.bfloat16, jnp.float32
    copies = 48
    return pl.pallas_call(
        kernel,
        out_shape=jax.ShapeDtypeStruct((2, 1, 2, ops, ops), f32),
        in_specs=[pl.BlockSpec(memory_space=pl.ANY)] * 2,
        out_specs=pl.BlockSpec(memory_space=pltpu.VMEM),
        scratch_shapes=[
            pltpu.VMEM((ops, 2, width, width), bf16),
            pltpu.VMEM((9, ops, 2, rows, width), bf16),
            pltpu.VMEM((UNITS, 2, width, width), bf16),
            pltpu.VMEM((2, UNITS, 2, rows, width), bf16),
            pltpu.VMEM((UNITS, 2, ops, rows, width), bf16),
            pltpu.VMEM((UNITS, 2, ops, rows, width), bf16),
            pltpu.VMEM((UNITS, 256, 256), f32),
            pltpu.VMEM((UNITS, 16, 256), f32),
            pltpu.VMEM((8, 2, 8, 128), f32),
            pltpu.VMEM((8, 2, 8, 128), f32),
            pltpu.VMEM((2, 8, 128), f32),
            pltpu.SemaphoreType.DMA((UNITS + 1,)),
            pltpu.SemaphoreType.DMA((copies,)),
            pltpu.SemaphoreType.DMA((copies,)),
            pltpu.SemaphoreType.DMA((8,)),
            pltpu.SemaphoreType.DMA((8,)),
            pltpu.SemaphoreType.DMA((2,)),
            pltpu.SemaphoreType.DMA((2,)),
        ],
        compiler_params=pltpu.CompilerParams(
            collective_id=0, has_side_effects=True, vmem_limit_bytes=62 * 2**20
        ),
        cost_estimate=pl.CostEstimate(
            flops=20 * 10**9, bytes_accessed=12 * 2**20, transcendentals=0
        ),
        name="correlate",
    )(perambulators, elements)


def solution(mesh):
    placed = (P("src", None, None, None, None), P("src", None, None, "snk", None))
    return jax.shard_map(
        on_device,
        mesh=mesh,
        in_specs=placed,
        out_specs=P(None, "src", "snk", None, None),
        check_vma=False,
    )
```

```python
import jax
import jax.numpy as jnp
from jax import lax
from jax.experimental import pallas as pl
from jax.experimental.pallas import tpu as pltpu
from jax.sharding import PartitionSpec as P

MESH = pl.DeviceIdType.MESH
UNITS = 9
NT_DIMS = (((1,), (1,)), ((), ()))

FLIP, NEXT, FLIP_PREV, HALF = 0, 1, 2, 3
SIB_OWN, SIB_FLIP, SIB_NEXT, SIB_FLIP_PREV, SIB_HALF = 4, 5, 6, 7, 8


ORDER = (
    "flip0", "flip1", "flip2", "flip3", "fore_tail", "back_tail", "fore_fifth", "back_fifth",
    "fore_head", "back_head", "next", "half_own", "sib", "S0", "Yx1", "S1", "pass_fifth",
    "yo0", "prev0", "yo1", "prev1", "yo2", "prev2", "yo3", "prev3", "half_flip", "sib_flip",
    "S2", "cross_b", "pass_tail", "cross_f", "fore_pair", "back_pair", "Yb1", "pass_head",
    "back_triple", "fore_triple", "Yx2", "Yf1", "sib_next", "S3", "sib_prev", "S5", "S4",
    "pass_pair", "S6", "cross_o", "sib_half", "S7", "pass_triple", "Yb2", "S8", "Yo1",
    "Yf2", "T1", "Yo2", "T2",
)


def dot(a, b):
    return jnp.dot(a, b, preferred_element_type=jnp.float32)


def dot_nt(a, b):
    return lax.dot_general(a, b, NT_DIMS, preferred_element_type=jnp.float32)


def exact_nt(a, b):
    return lax.dot_general(
        a, b, NT_DIMS, preferred_element_type=jnp.float32, precision=lax.Precision.HIGHEST
    )


def kernel(
    peram, elem, out, full, other, mats, left, xs, ys, gram, rowed, parts, sums, swapped,
    load_sem, send_sem, recv_sem, part_send, part_recv, swap_send, swap_recv,
):
    src = lax.axis_index("src")
    snk = lax.axis_index("snk")
    core = lax.rem(src, 2)
    z = lax.rem(src // 2, 4)
    ylo = src // 8
    x = snk // 2
    yhi = lax.rem(snk, 2)
    y = yhi * 2 + ylo
    tau = src // 2
    ops = elem.shape[1]
    rows = elem.shape[3]

    def place(px, py, pz, pc):
        return ((lax.rem(py, 2) * 4 + pz) * 2 + pc, px * 2 + py // 2)

    xf = lax.rem(x + 1 + 2 * core, 4)
    xb = lax.rem(x + 3 + 2 * core, 4)
    xo = lax.rem(x + 2, 4)
    yn = lax.rem(y + 1, 4)
    yp = lax.rem(y + 3, 4)
    yo = lax.rem(y + 2, 4)
    zn = lax.rem(z + 1, 4)
    zp = lax.rem(z + 3, 4)
    zo = lax.rem(z + 2, 4)
    yoh = yo // 2
    dev_fore = place(xf, y, z, core)
    dev_back = place(xb, y, z, core)
    dev_yo = place(x, yo, z, core)
    y_to = lax.rem(y + 3 + 2 * core, 4)
    y_from = lax.rem(y + 1 + 2 * core, 4)
    y_from_sib = lax.rem(y + 3 + 2 * core, 4)
    dev_flip = place(x, y_to, z, core)
    dev_flip_back = place(x, y_from, z, core)
    dev_zn = place(x, y, zn, core)
    dev_zp = place(x, y, zp, core)
    dev_zo = place(x, y, zo, core)
    dev_sib = (src + 1 - 2 * core, snk)

    own_rows = snk
    flip_rows = x * 2 + y_from // 2
    flip_rows_sib = x * 2 + y_from_sib // 2
    low = z < 2
    flip_tau = (1 - ylo) * 4 + z
    next_tau = ylo * 4 + zn
    prev_tau = (1 - ylo) * 4 + zp
    half_tau = jnp.where(low, ylo, 1 - ylo) * 4 + zo
    sib = 1 - core
    flip_core = lax.rem(core + ylo, 2)
    taus = [tau, tau, flip_tau, next_tau, next_tau, prev_tau, prev_tau, half_tau, half_tau]
    cores = [core, sib, flip_core, core, sib, core, sib, core, sib]
    blocks = [
        own_rows,
        own_rows,
        jnp.where(ylo == 0, flip_rows, flip_rows_sib),
        own_rows,
        own_rows,
        flip_rows,
        flip_rows_sib,
        jnp.where(low, own_rows, flip_rows),
        jnp.where(low, own_rows, flip_rows_sib),
    ]
    slots = [
        None, SIB_OWN, jnp.where(ylo == 0, FLIP, SIB_FLIP), NEXT, SIB_NEXT,
        FLIP_PREV, SIB_FLIP_PREV, HALF, SIB_HALF,
    ]

    own_slice = full.at[:, :, pl.ds(pl.multiple_of(snk * rows, rows), rows), :]
    own_load = pltpu.make_async_copy(elem.at[0], own_slice, load_sem.at[UNITS])
    own_load.start()
    loads = []
    for u in range(UNITS):
        load = pltpu.make_async_copy(
            peram.at[0, taus[u] * 2 + cores[u]], mats.at[u], load_sem.at[u]
        )
        load.start()
        loads.append(load)

    swapped[...] = jnp.zeros_like(swapped)

    barrier = pltpu.get_barrier_semaphore()
    for step in range(1, 8):
        pl.semaphore_signal(
            barrier, inc=1, device_id=(src, lax.rem(snk + step, 8)), device_id_type=MESH
        )
    for target in (dev_flip, dev_flip_back, dev_zn, dev_zp, dev_zo, dev_sib):
        pl.semaphore_signal(barrier, inc=1, device_id=target, device_id_type=MESH)
    outside = snk != tau

    @pl.when(outside)
    def _():
        for c in range(2):
            pl.semaphore_signal(barrier, inc=1, device_id=(snk * 2 + c, tau), device_id_type=MESH)

    pl.semaphore_wait(barrier, jnp.where(outside, 15, 13))

    quarters = ((0, 2), (2, 2), (4, 2), (6, 2))
    tail, fifth, head = (5, 3), (4, 1), (0, 4)
    pair, triple = (0, 2), (2, 3)

    def block(px, pyh, piece):
        start = pl.multiple_of((px * 2 + pyh) * rows, rows)
        return full.at[pl.ds(*piece), :, pl.ds(start, rows), :]

    def slot(index, piece=(0, ops)):
        return other.at[index, pl.ds(*piece)]

    def mine(piece=(0, ops)):
        return elem.at[0, pl.ds(*piece)]

    sends = {}
    flips = tuple("flip%d" % i for i in range(4))
    prevs = tuple("prev%d" % i for i in range(4))
    partners = tuple("yo%d" % i for i in range(4))
    for i, q in enumerate(quarters):
        sends[flips[i]] = ((), mine(q), slot(FLIP, q), dev_flip, slot(FLIP, q))
        sends[partners[i]] = (
            flips[i : i + 1], slot(FLIP, q), block(x, y_from // 2, q), dev_flip,
            block(x, yoh, q),
        )
        sends[prevs[i]] = (
            flips[i : i + 1], slot(FLIP, q), slot(FLIP_PREV, q), dev_zn, slot(FLIP_PREV, q)
        )
    for name, piece in (("tail", tail), ("fifth", fifth), ("head", head)):
        sends["fore_" + name] = (
            (), mine(piece), block(x, yhi, piece), dev_fore, block(xb, yhi, piece)
        )
        sends["back_" + name] = (
            (), mine(piece), block(x, yhi, piece), dev_back, block(xf, yhi, piece)
        )
    for name, piece, needs in (
        ("pair", pair, partners[0:1]), ("triple", triple, partners[1:3])
    ):
        here = block(x, yoh, piece)
        sends["fore_" + name] = (needs, here, here, dev_fore, block(xb, yoh, piece))
        sends["back_" + name] = (needs, here, here, dev_back, block(xf, yoh, piece))
    for name, side, px, pyh, piece, device in (
        ("tail", "fore_", xb, yhi, tail, dev_fore),
        ("fifth", "fore_", xb, yhi, fifth, dev_fore),
        ("head", "back_", xf, yhi, head, dev_back),
        ("pair", "fore_", xb, yoh, pair, dev_fore),
        ("triple", "back_", xf, yoh, triple, dev_back),
    ):
        here = block(px, pyh, piece)
        sends["pass_" + name] = ((side + name,), here, here, device, block(xo, pyh, piece))
    for name, needs, px in (
        ("cross_b", "fore_tail", xb), ("cross_f", "back_tail", xf), ("cross_o", "pass_tail", xo)
    ):
        here = block(px, yhi, tail)
        sends[name] = ((needs,), here, here, dev_yo, block(px, yoh, tail))
    sends["next"] = ((), mine(), slot(NEXT), dev_zp, slot(NEXT))
    sends["half"] = ((), mine(), slot(HALF), dev_zo, slot(HALF))
    for name, needs, source, target in (
        ("sib", (), mine(), SIB_OWN),
        ("sib_flip", flips, slot(FLIP), SIB_FLIP),
        ("sib_next", ("next",), slot(NEXT), SIB_NEXT),
        ("sib_prev", prevs, slot(FLIP_PREV), SIB_FLIP_PREV),
        ("sib_half", ("half",), slot(HALF), SIB_HALF),
    ):
        sends[name] = (needs, source, slot(target), dev_sib, slot(target))
    numbers = {name: i for i, name in enumerate(sends)}
    seen = set()

    def descriptor(name, source, target, device):
        i = numbers[name]
        return pltpu.make_async_remote_copy(
            src_ref=source, dst_ref=target, send_sem=send_sem.at[i], recv_sem=recv_sem.at[i],
            device_id=device, device_id_type=MESH,
        )

    def arrive(names):
        for name in names:
            if name not in seen:
                seen.add(name)
                landed = sends[name][4]
                descriptor(name, landed, landed, dev_sib).wait_recv()

    def send(name):
        needs, source, target, device, _ = sends[name]
        arrive(needs)
        descriptor(name, source, target, device).start()

    def send_half(when, source):
        @pl.when(when)
        def _():
            descriptor("half", source, slot(HALF), dev_zo).start()

    col = lax.broadcasted_iota(jnp.int32, (rows, 512), 1)
    lane_sign = jnp.where(col < 256, 1.0, -1.0) * jnp.where(x < 2, 1.0, -1.0)

    def prepare(u):
        loads[u].wait()
        start = pl.multiple_of(blocks[u] * rows, rows)
        re = mats[u, 0, pl.ds(start, rows), :].astype(jnp.float32) * lane_sign
        im = mats[u, 1, pl.ds(start, rows), :].astype(jnp.float32) * lane_sign
        left[0, u, 0] = re.astype(jnp.bfloat16)
        left[0, u, 1] = (-im).astype(jnp.bfloat16)
        left[1, u, 0] = im.astype(jnp.bfloat16)
        left[1, u, 1] = re.astype(jnp.bfloat16)

    def sink_product(u):
        if u == 0:
            start = pl.multiple_of(snk * rows, rows)
            er = full[:, 0, pl.ds(start, rows), :]
            ei = full[:, 1, pl.ds(start, rows), :]
        else:
            er = other[slots[u], :, 0]
            ei = other[slots[u], :, 1]
        e = jnp.concatenate(
            [er.reshape(ops * rows, 512), ei.reshape(ops * rows, 512)], axis=1
        )
        pr = mats[u, 0]
        pi = mats[u, 1]
        re = dot(e, jnp.concatenate([pr, -pi], axis=0))
        xs[u, 0] = re.astype(jnp.bfloat16).reshape(ops, rows, 512)
        im = dot(e, jnp.concatenate([pi, pr], axis=0))
        xs[u, 1] = im.astype(jnp.bfloat16).reshape(ops, rows, 512)

    lane = lax.broadcasted_iota(jnp.int32, (384, 128), 1)

    def source_product(px, pyh, first):
        cols = pl.ds(pl.multiple_of(px * 128, 128), 128)
        krows = pl.ds(pl.multiple_of((px * 2 + pyh) * rows, rows), rows)
        here = (lane // 64) == pyh
        for m in range(3):
            units = slice(3 * m, 3 * m + 3)
            a = jnp.concatenate(
                [left[0, units].reshape(384, 512), left[1, units].reshape(384, 512)], axis=1
            )
            for q in range(ops // 4):
                w = jnp.concatenate(
                    [full[4 * q : 4 * q + 4, c, krows, :].reshape(256, 512) for c in range(2)],
                    axis=1,
                )
                r = dot_nt(a, w)
                for j in range(2):
                    v = r[:, 128 * j : 128 * j + 128]
                    t = pltpu.roll(v, 64, 1)
                    for k, new in enumerate(
                        (jnp.where(lane < 64, v, t), jnp.where(lane < 64, t, v))
                    ):
                        o = q * 4 + 2 * j + k
                        new = new.astype(jnp.bfloat16)
                        if not first:
                            new = jnp.where(here, new, ys[units, :, o, :, cols].reshape(384, 128))
                        ys[units, :, o, :, cols] = new.reshape(3, 2, rows, 128)

    r_iota = lax.broadcasted_iota(jnp.int32, (256, 256), 0)
    c_iota = lax.broadcasted_iota(jnp.int32, (256, 256), 1)
    same = lax.rem(r_iota, 16) == lax.rem(c_iota, 16)

    def trace(columns, last):
        for u in range(UNITS):
            total = dot_nt(*(
                jnp.concatenate(
                    [
                        held[u, :, :, 16 * i : 16 * i + 16,
                             pl.ds(pl.multiple_of(px * 128, 128), 128)].reshape(256, 128)
                        for i in range(rows // 16)
                        for px in columns
                    ],
                    axis=1,
                )
                for held in (xs, ys)
            ))
            if last:
                total = jnp.where(same, total + gram[u], 0.0)
                rowed[u] = jnp.sum(total.reshape(2 * ops, 16, 256), axis=1)
            else:
                gram[u] = total

    sinks = (
        (), ("sib",), flips + ("sib_flip",), ("next",), ("sib_next",), prevs, ("sib_prev",),
        ("half",), ("sib_half",),
    )
    products = {
        "Yx1": (x, yhi, ()),
        "Yx2": (x, yoh, partners),
        "Yb1": (xb, yhi, ("fore_tail", "fore_fifth", "fore_head")),
        "Yf1": (xf, yhi, ("back_tail", "back_fifth", "back_head")),
        "Yo1": (xo, yhi, ("pass_tail", "pass_fifth", "pass_head")),
        "Yb2": (xb, yoh, ("fore_pair", "fore_triple", "cross_b")),
        "Yf2": (xf, yoh, ("back_pair", "back_triple", "cross_f")),
        "Yo2": (xo, yoh, ("pass_pair", "pass_triple", "cross_o")),
    }
    begun = set()
    for name in ORDER:
        if name in sends:
            send(name)
        elif name == "half_own":
            send_half(jnp.logical_not(low), mine())
        elif name == "half_flip":
            arrive(flips)
            send_half(low, slot(FLIP))
        elif name in products:
            px, pyh, needs = products[name]
            arrive(needs)
            source_product(px, pyh, name[1] not in begun)
            begun.add(name[1])
        elif name[0] == "S":
            if name == "S0":
                own_load.wait()
                for u in range(UNITS):
                    prepare(u)
            u = int(name[1])
            arrive(sinks[u])
            sink_product(u)
        elif name == "T1":
            trace((x, xf, xb), False)
        else:
            trace((xo,), True)

    parts[...] = jnp.zeros_like(parts)
    pick_row = lax.broadcasted_iota(jnp.int32, (16, 256), 0)
    pick_group = lax.broadcasted_iota(jnp.int32, (16, 256), 1) // 16
    straight = jnp.where(pick_row == pick_group, 1.0, 0.0)
    crossed = jnp.where(
        pick_row < 8,
        jnp.where(pick_group == pick_row + 8, -1.0, 0.0),
        jnp.where(pick_group == pick_row - 8, 1.0, 0.0),
    )
    traces = exact_nt(rowed[:, 0:8].reshape(UNITS * 8, 256), straight) + exact_nt(
        rowed[:, 8:16].reshape(UNITS * 8, 256), crossed
    )
    for u in range(UNITS):
        parts[taus[u], cores[u], :, 0:16] = traces[8 * u : 8 * u + 8]

    part_copies = []
    for step in range(1, 8):
        to = lax.rem(snk + step, 8)
        copy = pltpu.make_async_remote_copy(
            src_ref=parts.at[to], dst_ref=sums.at[step], send_sem=part_send.at[step],
            recv_sem=part_recv.at[step], device_id=(src, to), device_id_type=MESH,
        )
        copy.start()
        part_copies.append(copy)
    sums[0] = parts[snk]
    for copy in part_copies:
        copy.wait()
    sums[0] = jnp.sum(sums[...], axis=0)
    def swap_copy(c):
        return pltpu.make_async_remote_copy(
            src_ref=sums.at[0, c], dst_ref=swapped.at[core], send_sem=swap_send.at[c],
            recv_sem=swap_recv.at[core], device_id=(snk * 2 + c, tau), device_id_type=MESH,
        )

    @pl.when(outside)
    def _():
        for c in range(2):
            swap_copy(c).start()
        for c in range(2):
            swap_copy(c).wait_send()
            pltpu.make_async_remote_copy(
                src_ref=sums.at[0, c], dst_ref=swapped.at[c], send_sem=swap_send.at[c],
                recv_sem=swap_recv.at[c], device_id=(snk * 2 + c, tau), device_id_type=MESH,
            ).wait_recv()

    turn_row = lax.broadcasted_iota(jnp.int32, (8, 128), 0)
    turn_lane = lax.broadcasted_iota(jnp.int32, (8, 128), 1)
    for c in range(2):
        for part in range(2):
            turn = jnp.where(turn_lane == turn_row + 8 * part, 1.0, 0.0)
            out[part, 0, c] = sums[0, c, :, 8 * part : 8 * part + 8] + exact_nt(turn, swapped[c])
    for name, (_, source, target, device, _) in sends.items():
        descriptor(name, source, target, device).wait_send()


def on_device(perambulators, elements):
    ops, rows, width = elements.shape[1], elements.shape[3], elements.shape[4]
    bf16, f32 = jnp.bfloat16, jnp.float32
    copies = 48
    return pl.pallas_call(
        kernel,
        out_shape=jax.ShapeDtypeStruct((2, 1, 2, ops, ops), f32),
        in_specs=[pl.BlockSpec(memory_space=pl.ANY)] * 2,
        out_specs=pl.BlockSpec(memory_space=pltpu.VMEM),
        scratch_shapes=[
            pltpu.VMEM((ops, 2, width, width), bf16),
            pltpu.VMEM((9, ops, 2, rows, width), bf16),
            pltpu.VMEM((UNITS, 2, width, width), bf16),
            pltpu.VMEM((2, UNITS, 2, rows, width), bf16),
            pltpu.VMEM((UNITS, 2, ops, rows, width), bf16),
            pltpu.VMEM((UNITS, 2, ops, rows, width), bf16),
            pltpu.VMEM((UNITS, 256, 256), f32),
            pltpu.VMEM((UNITS, 16, 256), f32),
            pltpu.VMEM((8, 2, 8, 128), f32),
            pltpu.VMEM((8, 2, 8, 128), f32),
            pltpu.VMEM((2, 8, 128), f32),
            pltpu.SemaphoreType.DMA((UNITS + 1,)),
            pltpu.SemaphoreType.DMA((copies,)),
            pltpu.SemaphoreType.DMA((copies,)),
            pltpu.SemaphoreType.DMA((8,)),
            pltpu.SemaphoreType.DMA((8,)),
            pltpu.SemaphoreType.DMA((2,)),
            pltpu.SemaphoreType.DMA((2,)),
        ],
        compiler_params=pltpu.CompilerParams(
            collective_id=0, has_side_effects=True, vmem_limit_bytes=62 * 2**20
        ),
        cost_estimate=pl.CostEstimate(
            flops=20 * 10**9, bytes_accessed=12 * 2**20, transcendentals=0
        ),
        name="correlate",
    )(perambulators, elements)


def solution(mesh):
    placed = (P("src", None, None, None, None), P("src", None, None, "snk", None))
    return jax.shard_map(
        on_device,
        mesh=mesh,
        in_specs=placed,
        out_specs=P(None, "src", "snk", None, None),
        check_vma=False,
    )
```

```python
import jax
import jax.numpy as jnp
from jax import lax
from jax.experimental import pallas as pl
from jax.experimental.pallas import tpu as pltpu
from jax.sharding import PartitionSpec as P

MESH = pl.DeviceIdType.MESH
UNITS = 9
NT_DIMS = (((1,), (1,)), ((), ()))

FLIP, NEXT, FLIP_PREV, HALF = 0, 1, 2, 3
SIB_OWN, SIB_FLIP, SIB_NEXT, SIB_FLIP_PREV, SIB_HALF = 4, 5, 6, 7, 8


ORDER = (
    "flip0", "flip1", "flip2", "flip3", "fore_tail", "back_tail", "fore_fifth", "back_fifth",
    "fore_head", "back_head", "next", "sib", "S0", "yo0", "prev0", "yo1", "prev1", "yo2",
    "prev2", "pass_tail", "cross_b", "cross_f", "yo3", "prev3", "half_own", "half_flip",
    "pass_fifth", "Yx1", "sib_flip", "fore_pair", "back_pair", "S1", "S2", "back_triple",
    "fore_triple", "pass_head", "Yb1", "sib_next", "Yf1", "S3", "S4", "cross_o", "cross_o5",
    "pass_pair", "pass_twin", "Yx2", "Yf2", "sib_prev", "S5", "S6", "sib_half", "Yb2", "Yo1",
    "S7", "T1a", "S8", "T1b", "Yo2", "T2",
)


def dot(a, b):
    return jnp.dot(a, b, preferred_element_type=jnp.float32)


def dot_nt(a, b):
    return lax.dot_general(a, b, NT_DIMS, preferred_element_type=jnp.float32)


def exact_nt(a, b):
    return lax.dot_general(
        a, b, NT_DIMS, preferred_element_type=jnp.float32, precision=lax.Precision.HIGHEST
    )


def kernel(
    peram, elem, out, full, other, mats, left, xs, ys, gram, rowed, parts, sums, swapped,
    load_sem, send_sem, recv_sem, part_send, part_recv, swap_send, swap_recv,
):
    src = lax.axis_index("src")
    snk = lax.axis_index("snk")
    core = lax.rem(src, 2)
    z = lax.rem(src // 2, 4)
    ylo = src // 8
    x = snk // 2
    yhi = lax.rem(snk, 2)
    y = yhi * 2 + ylo
    tau = src // 2
    ops = elem.shape[1]
    rows = elem.shape[3]

    def place(px, py, pz, pc):
        return ((lax.rem(py, 2) * 4 + pz) * 2 + pc, px * 2 + py // 2)

    xf = lax.rem(x + 1 + 2 * core, 4)
    xb = lax.rem(x + 3 + 2 * core, 4)
    xo = lax.rem(x + 2, 4)
    yn = lax.rem(y + 1, 4)
    yp = lax.rem(y + 3, 4)
    yo = lax.rem(y + 2, 4)
    zn = lax.rem(z + 1, 4)
    zp = lax.rem(z + 3, 4)
    zo = lax.rem(z + 2, 4)
    yoh = yo // 2
    dev_fore = place(xf, y, z, core)
    dev_back = place(xb, y, z, core)
    dev_yo = place(x, yo, z, core)
    y_to = lax.rem(y + 3 + 2 * core, 4)
    y_from = lax.rem(y + 1 + 2 * core, 4)
    y_from_sib = lax.rem(y + 3 + 2 * core, 4)
    dev_flip = place(x, y_to, z, core)
    dev_flip_back = place(x, y_from, z, core)
    dev_zn = place(x, y, zn, core)
    dev_zp = place(x, y, zp, core)
    dev_zo = place(x, y, zo, core)
    dev_sib = (src + 1 - 2 * core, snk)

    own_rows = snk
    flip_rows = x * 2 + y_from // 2
    flip_rows_sib = x * 2 + y_from_sib // 2
    low = z < 2
    flip_tau = (1 - ylo) * 4 + z
    next_tau = ylo * 4 + zn
    prev_tau = (1 - ylo) * 4 + zp
    half_tau = jnp.where(low, ylo, 1 - ylo) * 4 + zo
    sib = 1 - core
    flip_core = lax.rem(core + ylo, 2)
    taus = [tau, tau, flip_tau, next_tau, next_tau, prev_tau, prev_tau, half_tau, half_tau]
    cores = [core, sib, flip_core, core, sib, core, sib, core, sib]
    blocks = [
        own_rows,
        own_rows,
        jnp.where(ylo == 0, flip_rows, flip_rows_sib),
        own_rows,
        own_rows,
        flip_rows,
        flip_rows_sib,
        jnp.where(low, own_rows, flip_rows),
        jnp.where(low, own_rows, flip_rows_sib),
    ]
    slots = [
        None, SIB_OWN, jnp.where(ylo == 0, FLIP, SIB_FLIP), NEXT, SIB_NEXT,
        FLIP_PREV, SIB_FLIP_PREV, HALF, SIB_HALF,
    ]

    own_slice = full.at[:, :, pl.ds(pl.multiple_of(snk * rows, rows), rows), :]
    own_load = pltpu.make_async_copy(elem.at[0], own_slice, load_sem.at[UNITS])
    own_load.start()
    loads = []
    for u in range(UNITS):
        load = pltpu.make_async_copy(
            peram.at[0, taus[u] * 2 + cores[u]], mats.at[u], load_sem.at[u]
        )
        load.start()
        loads.append(load)

    swapped[...] = jnp.zeros_like(swapped)

    barrier = pltpu.get_barrier_semaphore()
    for step in range(1, 8):
        pl.semaphore_signal(
            barrier, inc=1, device_id=(src, lax.rem(snk + step, 8)), device_id_type=MESH
        )
    for target in (dev_flip, dev_flip_back, dev_zn, dev_zp, dev_zo, dev_sib):
        pl.semaphore_signal(barrier, inc=1, device_id=target, device_id_type=MESH)
    def computed(c):
        whole = (snk == tau) | (snk == next_tau) | (snk == prev_tau) | (snk == half_tau)
        return whole | ((snk == flip_tau) & (flip_core == c))

    for c in range(2):
        @pl.when(jnp.logical_not(computed(c)))
        def _(c=c):
            for k in range(8):
                pl.semaphore_signal(
                    barrier, inc=1, device_id=(snk * 2 + c, k), device_id_type=MESH
                )

    pl.semaphore_wait(barrier, 13 + UNITS - 2)

    quarters = ((0, 2), (2, 2), (4, 2), (6, 2))
    tail, fifth, head = (5, 3), (4, 1), (0, 4)
    pair, triple, twin = (0, 2), (2, 3), (2, 2)

    def block(px, pyh, piece):
        start = pl.multiple_of((px * 2 + pyh) * rows, rows)
        return full.at[pl.ds(*piece), :, pl.ds(start, rows), :]

    def slot(index, piece=(0, ops)):
        return other.at[index, pl.ds(*piece)]

    def mine(piece=(0, ops)):
        return elem.at[0, pl.ds(*piece)]

    sends = {}
    flips = tuple("flip%d" % i for i in range(4))
    prevs = tuple("prev%d" % i for i in range(4))
    partners = tuple("yo%d" % i for i in range(4))
    for i, q in enumerate(quarters):
        sends[flips[i]] = ((), mine(q), slot(FLIP, q), dev_flip, slot(FLIP, q))
        sends[partners[i]] = (
            flips[i : i + 1], slot(FLIP, q), block(x, y_from // 2, q), dev_flip,
            block(x, yoh, q),
        )
        sends[prevs[i]] = (
            flips[i : i + 1], slot(FLIP, q), slot(FLIP_PREV, q), dev_zn, slot(FLIP_PREV, q)
        )
    for name, piece in (("tail", tail), ("fifth", fifth), ("head", head)):
        sends["fore_" + name] = (
            (), mine(piece), block(x, yhi, piece), dev_fore, block(xb, yhi, piece)
        )
        sends["back_" + name] = (
            (), mine(piece), block(x, yhi, piece), dev_back, block(xf, yhi, piece)
        )
    for name, piece, needs in (
        ("pair", pair, partners[0:1]), ("triple", triple, partners[1:3])
    ):
        here = block(x, yoh, piece)
        sends["fore_" + name] = (needs, here, here, dev_fore, block(xb, yoh, piece))
        sends["back_" + name] = (needs, here, here, dev_back, block(xf, yoh, piece))
    for name, side, px, pyh, piece, device in (
        ("tail", "fore_", xb, yhi, tail, dev_fore),
        ("fifth", "fore_", xb, yhi, fifth, dev_fore),
        ("head", "back_", xf, yhi, head, dev_back),
        ("pair", "fore_", xb, yoh, pair, dev_fore),
        ("twin", "back_", xf, yoh, twin, dev_back),
    ):
        here = block(px, pyh, piece)
        source = "triple" if piece is twin else name
        sends["pass_" + name] = ((side + source,), here, here, device, block(xo, pyh, piece))
    for name, needs, px, piece in (
        ("cross_b", "fore_tail", xb, tail),
        ("cross_f", "back_tail", xf, tail),
        ("cross_o", "pass_tail", xo, tail),
        ("cross_o5", "pass_fifth", xo, fifth),
    ):
        here = block(px, yhi, piece)
        sends[name] = ((needs,), here, here, dev_yo, block(px, yoh, piece))
    sends["next"] = ((), mine(), slot(NEXT), dev_zp, slot(NEXT))
    sends["half"] = ((), mine(), slot(HALF), dev_zo, slot(HALF))
    for name, needs, source, target in (
        ("sib", (), mine(), SIB_OWN),
        ("sib_flip", flips, slot(FLIP), SIB_FLIP),
        ("sib_next", ("next",), slot(NEXT), SIB_NEXT),
        ("sib_prev", prevs, slot(FLIP_PREV), SIB_FLIP_PREV),
        ("sib_half", ("half",), slot(HALF), SIB_HALF),
    ):
        sends[name] = (needs, source, slot(target), dev_sib, slot(target))
    numbers = {name: i for i, name in enumerate(sends)}
    seen = set()

    def descriptor(name, source, target, device):
        i = numbers[name]
        return pltpu.make_async_remote_copy(
            src_ref=source, dst_ref=target, send_sem=send_sem.at[i], recv_sem=recv_sem.at[i],
            device_id=device, device_id_type=MESH,
        )

    def arrive(names):
        for name in names:
            if name not in seen:
                seen.add(name)
                landed = sends[name][4]
                descriptor(name, landed, landed, dev_sib).wait_recv()

    def send(name):
        needs, source, target, device, _ = sends[name]
        arrive(needs)
        descriptor(name, source, target, device).start()

    def send_half(when, source):
        @pl.when(when)
        def _():
            descriptor("half", source, slot(HALF), dev_zo).start()

    col = lax.broadcasted_iota(jnp.int32, (rows, 512), 1)
    lane_sign = jnp.where(col < 256, 1.0, -1.0) * jnp.where(x < 2, 1.0, -1.0)

    def prepare(u):
        loads[u].wait()
        start = pl.multiple_of(blocks[u] * rows, rows)
        re = mats[u, 0, pl.ds(start, rows), :].astype(jnp.float32) * lane_sign
        im = mats[u, 1, pl.ds(start, rows), :].astype(jnp.float32) * lane_sign
        left[0, u, 0] = re.astype(jnp.bfloat16)
        left[0, u, 1] = (-im).astype(jnp.bfloat16)
        left[1, u, 0] = im.astype(jnp.bfloat16)
        left[1, u, 1] = re.astype(jnp.bfloat16)

    def sink_product(u):
        if u == 0:
            start = pl.multiple_of(snk * rows, rows)
            er = full[:, 0, pl.ds(start, rows), :]
            ei = full[:, 1, pl.ds(start, rows), :]
        else:
            er = other[slots[u], :, 0]
            ei = other[slots[u], :, 1]
        e = jnp.concatenate(
            [er.reshape(ops * rows, 512), ei.reshape(ops * rows, 512)], axis=1
        )
        pr = mats[u, 0]
        pi = mats[u, 1]
        re = dot(e, jnp.concatenate([pr, -pi], axis=0))
        xs[u, 0] = re.astype(jnp.bfloat16).reshape(ops, rows, 512)
        im = dot(e, jnp.concatenate([pi, pr], axis=0))
        xs[u, 1] = im.astype(jnp.bfloat16).reshape(ops, rows, 512)

    lane = lax.broadcasted_iota(jnp.int32, (384, 128), 1)

    def source_product(px, pyh, first):
        cols = pl.ds(pl.multiple_of(px * 128, 128), 128)
        krows = pl.ds(pl.multiple_of((px * 2 + pyh) * rows, rows), rows)
        here = (lane // 64) == pyh
        for m in range(3):
            units = slice(3 * m, 3 * m + 3)
            a = jnp.concatenate(
                [left[0, units].reshape(384, 512), left[1, units].reshape(384, 512)], axis=1
            )
            for q in range(ops // 4):
                w = jnp.concatenate(
                    [full[4 * q : 4 * q + 4, c, krows, :].reshape(256, 512) for c in range(2)],
                    axis=1,
                )
                r = dot_nt(a, w)
                for j in range(2):
                    v = r[:, 128 * j : 128 * j + 128]
                    t = pltpu.roll(v, 64, 1)
                    for k, new in enumerate(
                        (jnp.where(lane < 64, v, t), jnp.where(lane < 64, t, v))
                    ):
                        o = q * 4 + 2 * j + k
                        new = new.astype(jnp.bfloat16)
                        if not first:
                            new = jnp.where(here, new, ys[units, :, o, :, cols].reshape(384, 128))
                        ys[units, :, o, :, cols] = new.reshape(3, 2, rows, 128)

    r_iota = lax.broadcasted_iota(jnp.int32, (256, 256), 0)
    c_iota = lax.broadcasted_iota(jnp.int32, (256, 256), 1)
    same = lax.rem(r_iota, 16) == lax.rem(c_iota, 16)

    def trace(columns, units, last):
        for u in units:
            total = dot_nt(*(
                jnp.concatenate(
                    [
                        held[u, :, :, 16 * i : 16 * i + 16,
                             pl.ds(pl.multiple_of(px * 128, 128), 128)].reshape(256, 128)
                        for i in range(rows // 16)
                        for px in columns
                    ],
                    axis=1,
                )
                for held in (xs, ys)
            ))
            if last:
                total = jnp.where(same, total + gram[u], 0.0)
                rowed[u] = jnp.sum(total.reshape(2 * ops, 16, 256), axis=1)
            else:
                gram[u] = total

    sinks = (
        (), ("sib",), flips + ("sib_flip",), ("next",), ("sib_next",), prevs, ("sib_prev",),
        ("half",), ("sib_half",),
    )
    products = {
        "Yx1": (x, yhi, ()),
        "Yx2": (x, yoh, partners),
        "Yb1": (xb, yhi, ("fore_tail", "fore_fifth", "fore_head")),
        "Yf1": (xf, yhi, ("back_tail", "back_fifth", "back_head")),
        "Yo1": (xo, yhi, ("pass_tail", "pass_fifth", "pass_head")),
        "Yb2": (xb, yoh, ("fore_pair", "fore_triple", "cross_b")),
        "Yf2": (xf, yoh, ("back_pair", "back_triple", "cross_f")),
        "Yo2": (xo, yoh, ("pass_pair", "pass_twin", "cross_o", "cross_o5")),
    }
    begun = set()
    for name in ORDER:
        if name in sends:
            send(name)
        elif name == "half_own":
            send_half(jnp.logical_not(low), mine())
        elif name == "half_flip":
            arrive(flips)
            send_half(low, slot(FLIP))
        elif name in products:
            px, pyh, needs = products[name]
            arrive(needs)
            source_product(px, pyh, name[1] not in begun)
            begun.add(name[1])
        elif name[0] == "S":
            if name == "S0":
                own_load.wait()
                for u in range(UNITS):
                    prepare(u)
            u = int(name[1])
            arrive(sinks[u])
            sink_product(u)
        elif name == "T1a":
            trace((x, xf, xb), range(7), False)
        elif name == "T1b":
            trace((x, xf, xb), range(7, UNITS), False)
        else:
            trace((xo,), range(UNITS), True)

    parts[...] = jnp.zeros_like(parts)
    pick_row = lax.broadcasted_iota(jnp.int32, (16, 256), 0)
    pick_group = lax.broadcasted_iota(jnp.int32, (16, 256), 1) // 16
    straight = jnp.where(pick_row == pick_group, 1.0, 0.0)
    crossed = jnp.where(
        pick_row < 8,
        jnp.where(pick_group == pick_row + 8, -1.0, 0.0),
        jnp.where(pick_group == pick_row - 8, 1.0, 0.0),
    )
    traces = exact_nt(rowed[:, 0:8].reshape(UNITS * 8, 256), straight) + exact_nt(
        rowed[:, 8:16].reshape(UNITS * 8, 256), crossed
    )
    for u in range(UNITS):
        parts[taus[u], cores[u], :, 0:16] = traces[8 * u : 8 * u + 8]

    swap_copies = []
    for u in range(2, UNITS):
        copy = pltpu.make_async_remote_copy(
            src_ref=parts.at[taus[u], cores[u]], dst_ref=swapped.at[core, snk],
            send_sem=swap_send.at[u - 2], recv_sem=swap_recv.at[core, snk],
            device_id=(taus[u] * 2 + cores[u], tau), device_id_type=MESH,
        )
        copy.start()
        swap_copies.append(copy)
    part_copies = []
    for step in range(1, 8):
        to = lax.rem(snk + step, 8)
        copy = pltpu.make_async_remote_copy(
            src_ref=parts.at[to], dst_ref=sums.at[step], send_sem=part_send.at[step],
            recv_sem=part_recv.at[step], device_id=(src, to), device_id_type=MESH,
        )
        copy.start()
        part_copies.append(copy)
    sums[0] = parts[snk]
    for copy in part_copies:
        copy.wait()
    for c in range(2):
        @pl.when(jnp.logical_not(computed(c)))
        def _(c=c):
            for k in range(8):
                pltpu.make_async_remote_copy(
                    src_ref=swapped.at[c, k], dst_ref=swapped.at[c, k],
                    send_sem=swap_send.at[0], recv_sem=swap_recv.at[c, k],
                    device_id=dev_sib, device_id_type=MESH,
                ).wait_recv()
    for copy in swap_copies:
        copy.wait_send()

    turn_row = lax.broadcasted_iota(jnp.int32, (8, 128), 0)
    turn_lane = lax.broadcasted_iota(jnp.int32, (8, 128), 1)
    for c in range(2):
        total = jnp.sum(sums[:, c], axis=0)
        other_total = jnp.sum(swapped[c], axis=0)
        for part in range(2):
            turn = jnp.where(turn_lane == turn_row + 8 * part, 1.0, 0.0)
            out[part, 0, c] = total[:, 8 * part : 8 * part + 8] + exact_nt(turn, other_total)
    for name, (_, source, target, device, _) in sends.items():
        descriptor(name, source, target, device).wait_send()


def on_device(perambulators, elements):
    ops, rows, width = elements.shape[1], elements.shape[3], elements.shape[4]
    bf16, f32 = jnp.bfloat16, jnp.float32
    copies = 48
    return pl.pallas_call(
        kernel,
        out_shape=jax.ShapeDtypeStruct((2, 1, 2, ops, ops), f32),
        in_specs=[pl.BlockSpec(memory_space=pl.ANY)] * 2,
        out_specs=pl.BlockSpec(memory_space=pltpu.VMEM),
        scratch_shapes=[
            pltpu.VMEM((ops, 2, width, width), bf16),
            pltpu.VMEM((9, ops, 2, rows, width), bf16),
            pltpu.VMEM((UNITS, 2, width, width), bf16),
            pltpu.VMEM((2, UNITS, 2, rows, width), bf16),
            pltpu.VMEM((UNITS, 2, ops, rows, width), bf16),
            pltpu.VMEM((UNITS, 2, ops, rows, width), bf16),
            pltpu.VMEM((UNITS, 256, 256), f32),
            pltpu.VMEM((UNITS, 16, 256), f32),
            pltpu.VMEM((8, 2, 8, 128), f32),
            pltpu.VMEM((8, 2, 8, 128), f32),
            pltpu.VMEM((2, 8, 8, 128), f32),
            pltpu.SemaphoreType.DMA((UNITS + 1,)),
            pltpu.SemaphoreType.DMA((copies,)),
            pltpu.SemaphoreType.DMA((copies,)),
            pltpu.SemaphoreType.DMA((8,)),
            pltpu.SemaphoreType.DMA((8,)),
            pltpu.SemaphoreType.DMA((UNITS - 2,)),
            pltpu.SemaphoreType.DMA((2, 8)),
        ],
        compiler_params=pltpu.CompilerParams(
            collective_id=0, has_side_effects=True, vmem_limit_bytes=62 * 2**20
        ),
        cost_estimate=pl.CostEstimate(
            flops=20 * 10**9, bytes_accessed=12 * 2**20, transcendentals=0
        ),
        name="correlate",
    )(perambulators, elements)


def solution(mesh):
    placed = (P("src", None, None, None, None), P("src", None, None, "snk", None))
    return jax.shard_map(
        on_device,
        mesh=mesh,
        in_specs=placed,
        out_specs=P(None, "src", "snk", None, None),
        check_vma=False,
    )
```

```python
import jax
import jax.numpy as jnp
from jax import lax
from jax.experimental import pallas as pl
from jax.experimental.pallas import tpu as pltpu
from jax.sharding import PartitionSpec as P

MESH = pl.DeviceIdType.MESH
UNITS = 9
NT_DIMS = (((1,), (1,)), ((), ()))

FLIP, NEXT, FLIP_PREV, HALF = 0, 1, 2, 3
SIB_OWN, SIB_FLIP, SIB_NEXT, SIB_FLIP_PREV, SIB_HALF = 4, 5, 6, 7, 8


ORDER = (
    "flip0", "flip1", "flip2", "flip3", "fore_tail", "back_tail", "fore_fifth", "back_fifth",
    "fore_head", "back_head", "next", "sib", "S0", "yo0", "prev0", "yo1", "prev1", "yo2",
    "prev2", "pass_tail", "cross_b", "cross_f", "yo3", "prev3", "pass_fifth", "Yx1", "sib_flip",
    "fore_pair", "back_pair", "S1", "S2", "back_triple", "fore_triple", "pass_head", "Yb1",
    "sib_next", "half_own", "half_flip", "Yf1", "S3", "S4", "cross_o", "cross_o5", "pass_pair",
    "pass_twin", "sib_prev", "S5", "S6", "Yx2", "Yf2l", "Yf2u", "T1a", "Yb2u", "Yb2l", "Yo1",
    "sib_half", "S7", "S8", "T1b", "Yo2u", "Yo2l", "T2",
)


def dot(a, b):
    return jnp.dot(a, b, preferred_element_type=jnp.float32)


def dot_nt(a, b):
    return lax.dot_general(a, b, NT_DIMS, preferred_element_type=jnp.float32)


def exact_nt(a, b):
    return lax.dot_general(
        a, b, NT_DIMS, preferred_element_type=jnp.float32, precision=lax.Precision.HIGHEST
    )


def kernel(
    peram, elem, out, full, other, mats, left, xs, ys, gram, rowed, parts, sums, swapped,
    load_sem, send_sem, recv_sem, part_send, part_recv, swap_send, swap_recv,
):
    src = lax.axis_index("src")
    snk = lax.axis_index("snk")
    core = lax.rem(src, 2)
    z = lax.rem(src // 2, 4)
    ylo = src // 8
    x = snk // 2
    yhi = lax.rem(snk, 2)
    y = yhi * 2 + ylo
    tau = src // 2
    ops = elem.shape[1]
    rows = elem.shape[3]

    def place(px, py, pz, pc):
        return ((lax.rem(py, 2) * 4 + pz) * 2 + pc, px * 2 + py // 2)

    xf = lax.rem(x + 1 + 2 * core, 4)
    xb = lax.rem(x + 3 + 2 * core, 4)
    xo = lax.rem(x + 2, 4)
    yn = lax.rem(y + 1, 4)
    yp = lax.rem(y + 3, 4)
    yo = lax.rem(y + 2, 4)
    zn = lax.rem(z + 1, 4)
    zp = lax.rem(z + 3, 4)
    zo = lax.rem(z + 2, 4)
    yoh = yo // 2
    dev_fore = place(xf, y, z, core)
    dev_back = place(xb, y, z, core)
    dev_yo = place(x, yo, z, core)
    y_to = lax.rem(y + 3 + 2 * core, 4)
    y_from = lax.rem(y + 1 + 2 * core, 4)
    y_from_sib = lax.rem(y + 3 + 2 * core, 4)
    dev_flip = place(x, y_to, z, core)
    dev_flip_back = place(x, y_from, z, core)
    dev_zn = place(x, y, zn, core)
    dev_zp = place(x, y, zp, core)
    dev_zo = place(x, y, zo, core)
    dev_sib = (src + 1 - 2 * core, snk)

    own_rows = snk
    flip_rows = x * 2 + y_from // 2
    flip_rows_sib = x * 2 + y_from_sib // 2
    low = z < 2
    flip_tau = (1 - ylo) * 4 + z
    next_tau = ylo * 4 + zn
    prev_tau = (1 - ylo) * 4 + zp
    half_tau = jnp.where(low, ylo, 1 - ylo) * 4 + zo
    sib = 1 - core
    flip_core = lax.rem(core + ylo, 2)
    taus = [tau, tau, flip_tau, next_tau, next_tau, prev_tau, prev_tau, half_tau, half_tau]
    cores = [core, sib, flip_core, core, sib, core, sib, core, sib]
    blocks = [
        own_rows,
        own_rows,
        jnp.where(ylo == 0, flip_rows, flip_rows_sib),
        own_rows,
        own_rows,
        flip_rows,
        flip_rows_sib,
        jnp.where(low, own_rows, flip_rows),
        jnp.where(low, own_rows, flip_rows_sib),
    ]
    slots = [
        None, SIB_OWN, jnp.where(ylo == 0, FLIP, SIB_FLIP), NEXT, SIB_NEXT,
        FLIP_PREV, SIB_FLIP_PREV, HALF, SIB_HALF,
    ]

    swapped[...] = jnp.zeros_like(swapped)

    barrier = pltpu.get_barrier_semaphore()
    for step in range(1, 8):
        pl.semaphore_signal(
            barrier, inc=1, device_id=(src, lax.rem(snk + step, 8)), device_id_type=MESH
        )
    for target in (dev_flip, dev_flip_back, dev_zn, dev_zp, dev_zo, dev_sib):
        pl.semaphore_signal(barrier, inc=1, device_id=target, device_id_type=MESH)
    def computed(c):
        whole = (snk == tau) | (snk == next_tau) | (snk == prev_tau) | (snk == half_tau)
        return whole | ((snk == flip_tau) & (flip_core == c))

    for c in range(2):
        @pl.when(jnp.logical_not(computed(c)))
        def _(c=c):
            for k in range(8):
                pl.semaphore_signal(
                    barrier, inc=1, device_id=(snk * 2 + c, k), device_id_type=MESH
                )

    own_slice = full.at[:, :, pl.ds(pl.multiple_of(snk * rows, rows), rows), :]
    own_load = pltpu.make_async_copy(elem.at[0], own_slice, load_sem.at[UNITS])
    own_load.start()
    loads = []
    for u in range(UNITS):
        load = pltpu.make_async_copy(
            peram.at[0, taus[u] * 2 + cores[u]], mats.at[u], load_sem.at[u]
        )
        load.start()
        loads.append(load)

    pl.semaphore_wait(barrier, 13 + UNITS - 2)

    quarters = ((0, 2), (2, 2), (4, 2), (6, 2))
    tail, fifth, head = (5, 3), (4, 1), (0, 4)
    pair, triple, twin = (0, 2), (2, 3), (2, 2)

    def block(px, pyh, piece):
        start = pl.multiple_of((px * 2 + pyh) * rows, rows)
        return full.at[pl.ds(*piece), :, pl.ds(start, rows), :]

    def slot(index, piece=(0, ops)):
        return other.at[index, pl.ds(*piece)]

    def mine(piece=(0, ops)):
        return elem.at[0, pl.ds(*piece)]

    sends = {}
    flips = tuple("flip%d" % i for i in range(4))
    prevs = tuple("prev%d" % i for i in range(4))
    partners = tuple("yo%d" % i for i in range(4))
    for i, q in enumerate(quarters):
        sends[flips[i]] = ((), mine(q), slot(FLIP, q), dev_flip, slot(FLIP, q))
        sends[partners[i]] = (
            flips[i : i + 1], slot(FLIP, q), block(x, y_from // 2, q), dev_flip,
            block(x, yoh, q),
        )
        sends[prevs[i]] = (
            flips[i : i + 1], slot(FLIP, q), slot(FLIP_PREV, q), dev_zn, slot(FLIP_PREV, q)
        )
    for name, piece in (("tail", tail), ("fifth", fifth), ("head", head)):
        sends["fore_" + name] = (
            (), mine(piece), block(x, yhi, piece), dev_fore, block(xb, yhi, piece)
        )
        sends["back_" + name] = (
            (), mine(piece), block(x, yhi, piece), dev_back, block(xf, yhi, piece)
        )
    for name, piece, needs in (
        ("pair", pair, partners[0:1]), ("triple", triple, partners[1:3])
    ):
        here = block(x, yoh, piece)
        sends["fore_" + name] = (needs, here, here, dev_fore, block(xb, yoh, piece))
        sends["back_" + name] = (needs, here, here, dev_back, block(xf, yoh, piece))
    for name, side, px, pyh, piece, device in (
        ("tail", "fore_", xb, yhi, tail, dev_fore),
        ("fifth", "fore_", xb, yhi, fifth, dev_fore),
        ("head", "back_", xf, yhi, head, dev_back),
        ("pair", "fore_", xb, yoh, pair, dev_fore),
        ("twin", "back_", xf, yoh, twin, dev_back),
    ):
        here = block(px, pyh, piece)
        source = "triple" if piece is twin else name
        sends["pass_" + name] = ((side + source,), here, here, device, block(xo, pyh, piece))
    for name, needs, px, piece in (
        ("cross_b", "fore_tail", xb, tail),
        ("cross_f", "back_tail", xf, tail),
        ("cross_o", "pass_tail", xo, tail),
        ("cross_o5", "pass_fifth", xo, fifth),
    ):
        here = block(px, yhi, piece)
        sends[name] = ((needs,), here, here, dev_yo, block(px, yoh, piece))
    sends["next"] = ((), mine(), slot(NEXT), dev_zp, slot(NEXT))
    sends["half"] = ((), mine(), slot(HALF), dev_zo, slot(HALF))
    for name, needs, source, target in (
        ("sib", (), mine(), SIB_OWN),
        ("sib_flip", flips, slot(FLIP), SIB_FLIP),
        ("sib_next", ("next",), slot(NEXT), SIB_NEXT),
        ("sib_prev", prevs, slot(FLIP_PREV), SIB_FLIP_PREV),
        ("sib_half", ("half",), slot(HALF), SIB_HALF),
    ):
        sends[name] = (needs, source, slot(target), dev_sib, slot(target))
    numbers = {name: i for i, name in enumerate(sends)}
    seen = set()

    def descriptor(name, source, target, device):
        i = numbers[name]
        return pltpu.make_async_remote_copy(
            src_ref=source, dst_ref=target, send_sem=send_sem.at[i], recv_sem=recv_sem.at[i],
            device_id=device, device_id_type=MESH,
        )

    def arrive(names):
        for name in names:
            if name not in seen:
                seen.add(name)
                landed = sends[name][4]
                descriptor(name, landed, landed, dev_sib).wait_recv()

    def send(name):
        needs, source, target, device, _ = sends[name]
        arrive(needs)
        descriptor(name, source, target, device).start()

    def send_half(when, source):
        @pl.when(when)
        def _():
            descriptor("half", source, slot(HALF), dev_zo).start()

    col = lax.broadcasted_iota(jnp.int32, (rows, 512), 1)
    lane_sign = jnp.where(col < 256, 1.0, -1.0) * jnp.where(x < 2, 1.0, -1.0)

    def prepare(u):
        loads[u].wait()
        start = pl.multiple_of(blocks[u] * rows, rows)
        re = mats[u, 0, pl.ds(start, rows), :].astype(jnp.float32) * lane_sign
        im = mats[u, 1, pl.ds(start, rows), :].astype(jnp.float32) * lane_sign
        left[0, u, 0] = re.astype(jnp.bfloat16)
        left[0, u, 1] = (-im).astype(jnp.bfloat16)
        left[1, u, 0] = im.astype(jnp.bfloat16)
        left[1, u, 1] = re.astype(jnp.bfloat16)

    def sink_product(u):
        if u == 0:
            start = pl.multiple_of(snk * rows, rows)
            er = full[:, 0, pl.ds(start, rows), :]
            ei = full[:, 1, pl.ds(start, rows), :]
        else:
            er = other[slots[u], :, 0]
            ei = other[slots[u], :, 1]
        e = jnp.concatenate(
            [er.reshape(ops * rows, 512), ei.reshape(ops * rows, 512)], axis=1
        )
        pr = mats[u, 0]
        pi = mats[u, 1]
        re = dot(e, jnp.concatenate([pr, -pi], axis=0))
        xs[u, 0] = re.astype(jnp.bfloat16).reshape(ops, rows, 512)
        im = dot(e, jnp.concatenate([pi, pr], axis=0))
        xs[u, 1] = im.astype(jnp.bfloat16).reshape(ops, rows, 512)

    lane = lax.broadcasted_iota(jnp.int32, (384, 128), 1)

    def source_product(px, pyh, first, groups):
        cols = pl.ds(pl.multiple_of(px * 128, 128), 128)
        krows = pl.ds(pl.multiple_of((px * 2 + pyh) * rows, rows), rows)
        here = (lane // 64) == pyh
        for m in range(3):
            units = slice(3 * m, 3 * m + 3)
            a = jnp.concatenate(
                [left[0, units].reshape(384, 512), left[1, units].reshape(384, 512)], axis=1
            )
            for q in groups:
                w = jnp.concatenate(
                    [full[4 * q : 4 * q + 4, c, krows, :].reshape(256, 512) for c in range(2)],
                    axis=1,
                )
                r = dot_nt(a, w)
                for j in range(2):
                    v = r[:, 128 * j : 128 * j + 128]
                    t = pltpu.roll(v, 64, 1)
                    for k, new in enumerate(
                        (jnp.where(lane < 64, v, t), jnp.where(lane < 64, t, v))
                    ):
                        o = q * 4 + 2 * j + k
                        new = new.astype(jnp.bfloat16)
                        if not first:
                            new = jnp.where(here, new, ys[units, :, o, :, cols].reshape(384, 128))
                        ys[units, :, o, :, cols] = new.reshape(3, 2, rows, 128)

    r_iota = lax.broadcasted_iota(jnp.int32, (256, 256), 0)
    c_iota = lax.broadcasted_iota(jnp.int32, (256, 256), 1)
    same = lax.rem(r_iota, 16) == lax.rem(c_iota, 16)

    def trace(columns, units, last):
        for u in units:
            total = dot_nt(*(
                jnp.concatenate(
                    [
                        held[u, :, :, 16 * i : 16 * i + 16,
                             pl.ds(pl.multiple_of(px * 128, 128), 128)].reshape(256, 128)
                        for i in range(rows // 16)
                        for px in columns
                    ],
                    axis=1,
                )
                for held in (xs, ys)
            ))
            if last:
                total = jnp.where(same, total + gram[u], 0.0)
                rowed[u] = jnp.sum(total.reshape(2 * ops, 16, 256), axis=1)
            else:
                gram[u] = total

    sinks = (
        (), ("sib",), flips + ("sib_flip",), ("next",), ("sib_next",), prevs, ("sib_prev",),
        ("half",), ("sib_half",),
    )
    both = (0, 1)
    products = {
        "Yx1": (x, yhi, both, ()),
        "Yx2": (x, yoh, both, partners),
        "Yb1": (xb, yhi, both, ("fore_tail", "fore_fifth", "fore_head")),
        "Yf1": (xf, yhi, both, ("back_tail", "back_fifth", "back_head")),
        "Yo1": (xo, yhi, both, ("pass_tail", "pass_fifth", "pass_head")),
        "Yb2u": (xb, yoh, (1,), ("fore_triple", "cross_b")),
        "Yb2l": (xb, yoh, (0,), ("fore_pair", "fore_triple")),
        "Yf2u": (xf, yoh, (1,), ("back_triple", "cross_f")),
        "Yf2l": (xf, yoh, (0,), ("back_pair", "back_triple")),
        "Yo2u": (xo, yoh, (1,), ("cross_o", "cross_o5")),
        "Yo2l": (xo, yoh, (0,), ("pass_pair", "pass_twin")),
    }
    for name in ORDER:
        if name in sends:
            send(name)
        elif name == "half_own":
            send_half(jnp.logical_not(low), mine())
        elif name == "half_flip":
            arrive(flips)
            send_half(low, slot(FLIP))
        elif name in products:
            px, pyh, groups, needs = products[name]
            arrive(needs)
            source_product(px, pyh, name[2] == "1", groups)
        elif name[0] == "S":
            if name == "S0":
                own_load.wait()
                for u in range(UNITS):
                    prepare(u)
            u = int(name[1])
            arrive(sinks[u])
            sink_product(u)
        elif name == "T1a":
            trace((x, xf), range(7), False)
        elif name == "T1b":
            trace((x, xf), range(7, UNITS), False)
        else:
            trace((xb, xo), range(UNITS), True)

    parts[...] = jnp.zeros_like(parts)
    pick_row = lax.broadcasted_iota(jnp.int32, (16, 256), 0)
    pick_group = lax.broadcasted_iota(jnp.int32, (16, 256), 1) // 16
    straight = jnp.where(pick_row == pick_group, 1.0, 0.0)
    crossed = jnp.where(
        pick_row < 8,
        jnp.where(pick_group == pick_row + 8, -1.0, 0.0),
        jnp.where(pick_group == pick_row - 8, 1.0, 0.0),
    )
    traces = exact_nt(rowed[:, 0:8].reshape(UNITS * 8, 256), straight) + exact_nt(
        rowed[:, 8:16].reshape(UNITS * 8, 256), crossed
    )
    for u in range(UNITS):
        parts[taus[u], cores[u], :, 0:16] = traces[8 * u : 8 * u + 8]

    swap_copies = []
    for u in range(2, UNITS):
        copy = pltpu.make_async_remote_copy(
            src_ref=parts.at[taus[u], cores[u]], dst_ref=swapped.at[core, snk],
            send_sem=swap_send.at[u - 2], recv_sem=swap_recv.at[core, snk],
            device_id=(taus[u] * 2 + cores[u], tau), device_id_type=MESH,
        )
        copy.start()
        swap_copies.append(copy)
    part_copies = []
    for step in range(1, 8):
        to = lax.rem(snk + step, 8)
        copy = pltpu.make_async_remote_copy(
            src_ref=parts.at[to], dst_ref=sums.at[step], send_sem=part_send.at[step],
            recv_sem=part_recv.at[step], device_id=(src, to), device_id_type=MESH,
        )
        copy.start()
        part_copies.append(copy)
    sums[0] = parts[snk]
    for copy in part_copies:
        copy.wait()
    for c in range(2):
        @pl.when(jnp.logical_not(computed(c)))
        def _(c=c):
            for k in range(8):
                pltpu.make_async_remote_copy(
                    src_ref=swapped.at[c, k], dst_ref=swapped.at[c, k],
                    send_sem=swap_send.at[0], recv_sem=swap_recv.at[c, k],
                    device_id=dev_sib, device_id_type=MESH,
                ).wait_recv()
    for copy in swap_copies:
        copy.wait_send()

    turn_row = lax.broadcasted_iota(jnp.int32, (8, 128), 0)
    turn_lane = lax.broadcasted_iota(jnp.int32, (8, 128), 1)
    for c in range(2):
        total = jnp.sum(sums[:, c], axis=0)
        other_total = jnp.sum(swapped[c], axis=0)
        for part in range(2):
            turn = jnp.where(turn_lane == turn_row + 8 * part, 1.0, 0.0)
            out[part, 0, c] = total[:, 8 * part : 8 * part + 8] + exact_nt(turn, other_total)
    for name, (_, source, target, device, _) in sends.items():
        descriptor(name, source, target, device).wait_send()


def on_device(perambulators, elements):
    ops, rows, width = elements.shape[1], elements.shape[3], elements.shape[4]
    bf16, f32 = jnp.bfloat16, jnp.float32
    copies = 48
    return pl.pallas_call(
        kernel,
        out_shape=jax.ShapeDtypeStruct((2, 1, 2, ops, ops), f32),
        in_specs=[pl.BlockSpec(memory_space=pl.ANY)] * 2,
        out_specs=pl.BlockSpec(memory_space=pltpu.VMEM),
        scratch_shapes=[
            pltpu.VMEM((ops, 2, width, width), bf16),
            pltpu.VMEM((9, ops, 2, rows, width), bf16),
            pltpu.VMEM((UNITS, 2, width, width), bf16),
            pltpu.VMEM((2, UNITS, 2, rows, width), bf16),
            pltpu.VMEM((UNITS, 2, ops, rows, width), bf16),
            pltpu.VMEM((UNITS, 2, ops, rows, width), bf16),
            pltpu.VMEM((UNITS, 256, 256), f32),
            pltpu.VMEM((UNITS, 16, 256), f32),
            pltpu.VMEM((8, 2, 8, 128), f32),
            pltpu.VMEM((8, 2, 8, 128), f32),
            pltpu.VMEM((2, 8, 8, 128), f32),
            pltpu.SemaphoreType.DMA((UNITS + 1,)),
            pltpu.SemaphoreType.DMA((copies,)),
            pltpu.SemaphoreType.DMA((copies,)),
            pltpu.SemaphoreType.DMA((8,)),
            pltpu.SemaphoreType.DMA((8,)),
            pltpu.SemaphoreType.DMA((UNITS - 2,)),
            pltpu.SemaphoreType.DMA((2, 8)),
        ],
        compiler_params=pltpu.CompilerParams(
            collective_id=0, has_side_effects=True, vmem_limit_bytes=62 * 2**20
        ),
        cost_estimate=pl.CostEstimate(
            flops=20 * 10**9, bytes_accessed=12 * 2**20, transcendentals=0
        ),
        name="correlate",
    )(perambulators, elements)


def solution(mesh):
    placed = (P("src", None, None, None, None), P("src", None, None, "snk", None))
    return jax.shard_map(
        on_device,
        mesh=mesh,
        in_specs=placed,
        out_specs=P(None, "src", "snk", None, None),
        check_vma=False,
    )
```

```python
import jax
import jax.numpy as jnp
from jax import lax
from jax.experimental import pallas as pl
from jax.experimental.pallas import tpu as pltpu
from jax.sharding import PartitionSpec as P

MESH = pl.DeviceIdType.MESH
UNITS = 9
NT_DIMS = (((1,), (1,)), ((), ()))

FLIP, NEXT, FLIP_PREV, HALF = 0, 1, 2, 3
SIB_OWN, SIB_FLIP, SIB_NEXT, SIB_FLIP_PREV, SIB_HALF = 4, 5, 6, 7, 8


ORDER = (
    "flip0", "flip1", "flip2", "flip3", "fore_tail", "back_tail", "fore_fifth", "back_fifth",
    "fore_head", "back_head", "next", "sib", "S0", "yo0", "prev0", "yo1", "prev1", "yo2",
    "prev2", "pass_tail", "cross_b", "cross_f", "yo3", "prev3", "pass_fifth", "Yx1", "sib_flip",
    "fore_pair", "back_pair", "S1", "S2", "back_triple", "fore_triple", "pass_head", "Yb1",
    "sib_next", "half_own", "half_flip", "Yf1", "S3", "S4", "cross_o", "sib_prev", "S5",
    "cross_o5", "S6", "pass_pair", "pass_twin", "Yx2", "Yf2l", "Yf2u", "T1a", "Yb2u",
    "sib_half", "Yb2l", "S7", "S8", "Yo1", "T1b", "Yo2u", "Yo2l", "T2",
)


def dot(a, b):
    return jnp.dot(a, b, preferred_element_type=jnp.float32)


def dot_nt(a, b):
    return lax.dot_general(a, b, NT_DIMS, preferred_element_type=jnp.float32)


def exact_nt(a, b):
    return lax.dot_general(
        a, b, NT_DIMS, preferred_element_type=jnp.float32, precision=lax.Precision.HIGHEST
    )


def kernel(
    peram, elem, out, full, other, mats, left, xs, ys, gram, rowed, parts, sums, swapped,
    load_sem, send_sem, recv_sem, part_send, part_recv, swap_send, swap_recv,
):
    src = lax.axis_index("src")
    snk = lax.axis_index("snk")
    core = lax.rem(src, 2)
    z = lax.rem(src // 2, 4)
    ylo = src // 8
    x = snk // 2
    yhi = lax.rem(snk, 2)
    y = yhi * 2 + ylo
    tau = src // 2
    ops = elem.shape[1]
    rows = elem.shape[3]

    def place(px, py, pz, pc):
        return ((lax.rem(py, 2) * 4 + pz) * 2 + pc, px * 2 + py // 2)

    xf = lax.rem(x + 1 + 2 * core, 4)
    xb = lax.rem(x + 3 + 2 * core, 4)
    xo = lax.rem(x + 2, 4)
    yn = lax.rem(y + 1, 4)
    yp = lax.rem(y + 3, 4)
    yo = lax.rem(y + 2, 4)
    zn = lax.rem(z + 1, 4)
    zp = lax.rem(z + 3, 4)
    zo = lax.rem(z + 2, 4)
    yoh = yo // 2
    dev_fore = place(xf, y, z, core)
    dev_back = place(xb, y, z, core)
    dev_yo = place(x, yo, z, core)
    y_to = lax.rem(y + 3 + 2 * core, 4)
    y_from = lax.rem(y + 1 + 2 * core, 4)
    y_from_sib = lax.rem(y + 3 + 2 * core, 4)
    dev_flip = place(x, y_to, z, core)
    dev_flip_back = place(x, y_from, z, core)
    dev_zn = place(x, y, zn, core)
    dev_zp = place(x, y, zp, core)
    dev_zo = place(x, y, zo, core)
    dev_sib = (src + 1 - 2 * core, snk)

    own_rows = snk
    flip_rows = x * 2 + y_from // 2
    flip_rows_sib = x * 2 + y_from_sib // 2
    low = z < 2
    flip_tau = (1 - ylo) * 4 + z
    next_tau = ylo * 4 + zn
    prev_tau = (1 - ylo) * 4 + zp
    half_tau = jnp.where(low, ylo, 1 - ylo) * 4 + zo
    sib = 1 - core
    flip_core = lax.rem(core + ylo, 2)
    taus = [tau, tau, flip_tau, next_tau, next_tau, prev_tau, prev_tau, half_tau, half_tau]
    cores = [core, sib, flip_core, core, sib, core, sib, core, sib]
    blocks = [
        own_rows,
        own_rows,
        jnp.where(ylo == 0, flip_rows, flip_rows_sib),
        own_rows,
        own_rows,
        flip_rows,
        flip_rows_sib,
        jnp.where(low, own_rows, flip_rows),
        jnp.where(low, own_rows, flip_rows_sib),
    ]
    slots = [
        None, SIB_OWN, jnp.where(ylo == 0, FLIP, SIB_FLIP), NEXT, SIB_NEXT,
        FLIP_PREV, SIB_FLIP_PREV, HALF, SIB_HALF,
    ]

    swapped[...] = jnp.zeros_like(swapped)

    barrier = pltpu.get_barrier_semaphore()
    for step in range(1, 8):
        pl.semaphore_signal(
            barrier, inc=1, device_id=(src, lax.rem(snk + step, 8)), device_id_type=MESH
        )
    for target in (dev_flip, dev_flip_back, dev_zn, dev_zp, dev_zo, dev_sib):
        pl.semaphore_signal(barrier, inc=1, device_id=target, device_id_type=MESH)
    def computed(c):
        whole = (snk == tau) | (snk == next_tau) | (snk == prev_tau) | (snk == half_tau)
        return whole | ((snk == flip_tau) & (flip_core == c))

    for c in range(2):
        @pl.when(jnp.logical_not(computed(c)))
        def _(c=c):
            for k in range(8):
                pl.semaphore_signal(
                    barrier, inc=1, device_id=(snk * 2 + c, k), device_id_type=MESH
                )

    own_slice = full.at[:, :, pl.ds(pl.multiple_of(snk * rows, rows), rows), :]
    own_load = pltpu.make_async_copy(elem.at[0], own_slice, load_sem.at[UNITS])
    own_load.start()
    loads = []
    for u in range(UNITS):
        load = pltpu.make_async_copy(
            peram.at[0, taus[u] * 2 + cores[u]], mats.at[u], load_sem.at[u]
        )
        load.start()
        loads.append(load)

    pl.semaphore_wait(barrier, 13 + UNITS - 2)

    quarters = ((0, 2), (2, 2), (4, 2), (6, 2))
    tail, fifth, head = (5, 3), (4, 1), (0, 4)
    pair, triple, twin = (0, 2), (2, 3), (2, 2)

    def block(px, pyh, piece):
        start = pl.multiple_of((px * 2 + pyh) * rows, rows)
        return full.at[pl.ds(*piece), :, pl.ds(start, rows), :]

    def slot(index, piece=(0, ops)):
        return other.at[index, pl.ds(*piece)]

    def mine(piece=(0, ops)):
        return elem.at[0, pl.ds(*piece)]

    sends = {}
    flips = tuple("flip%d" % i for i in range(4))
    prevs = tuple("prev%d" % i for i in range(4))
    partners = tuple("yo%d" % i for i in range(4))
    for i, q in enumerate(quarters):
        sends[flips[i]] = ((), mine(q), slot(FLIP, q), dev_flip, slot(FLIP, q))
        sends[partners[i]] = (
            flips[i : i + 1], slot(FLIP, q), block(x, y_from // 2, q), dev_flip,
            block(x, yoh, q),
        )
        sends[prevs[i]] = (
            flips[i : i + 1], slot(FLIP, q), slot(FLIP_PREV, q), dev_zn, slot(FLIP_PREV, q)
        )
    for name, piece in (("tail", tail), ("fifth", fifth), ("head", head)):
        sends["fore_" + name] = (
            (), mine(piece), block(x, yhi, piece), dev_fore, block(xb, yhi, piece)
        )
        sends["back_" + name] = (
            (), mine(piece), block(x, yhi, piece), dev_back, block(xf, yhi, piece)
        )
    for name, piece, needs in (
        ("pair", pair, partners[0:1]), ("triple", triple, partners[1:3])
    ):
        here = block(x, yoh, piece)
        sends["fore_" + name] = (needs, here, here, dev_fore, block(xb, yoh, piece))
        sends["back_" + name] = (needs, here, here, dev_back, block(xf, yoh, piece))
    for name, side, px, pyh, piece, device in (
        ("tail", "fore_", xb, yhi, tail, dev_fore),
        ("fifth", "fore_", xb, yhi, fifth, dev_fore),
        ("head", "back_", xf, yhi, head, dev_back),
        ("pair", "fore_", xb, yoh, pair, dev_fore),
        ("twin", "back_", xf, yoh, twin, dev_back),
    ):
        here = block(px, pyh, piece)
        source = "triple" if piece is twin else name
        sends["pass_" + name] = ((side + source,), here, here, device, block(xo, pyh, piece))
    for name, needs, px, piece in (
        ("cross_b", "fore_tail", xb, tail),
        ("cross_f", "back_tail", xf, tail),
        ("cross_o", "pass_tail", xo, tail),
        ("cross_o5", "pass_fifth", xo, fifth),
    ):
        here = block(px, yhi, piece)
        sends[name] = ((needs,), here, here, dev_yo, block(px, yoh, piece))
    sends["next"] = ((), mine(), slot(NEXT), dev_zp, slot(NEXT))
    sends["half"] = ((), mine(), slot(HALF), dev_zo, slot(HALF))
    for name, needs, source, target in (
        ("sib", (), mine(), SIB_OWN),
        ("sib_flip", flips, slot(FLIP), SIB_FLIP),
        ("sib_next", ("next",), slot(NEXT), SIB_NEXT),
        ("sib_prev", prevs, slot(FLIP_PREV), SIB_FLIP_PREV),
        ("sib_half", ("half",), slot(HALF), SIB_HALF),
    ):
        sends[name] = (needs, source, slot(target), dev_sib, slot(target))
    numbers = {name: i for i, name in enumerate(sends)}
    seen = set()

    def descriptor(name, source, target, device):
        i = numbers[name]
        return pltpu.make_async_remote_copy(
            src_ref=source, dst_ref=target, send_sem=send_sem.at[i], recv_sem=recv_sem.at[i],
            device_id=device, device_id_type=MESH,
        )

    def arrive(names):
        for name in names:
            if name not in seen:
                seen.add(name)
                landed = sends[name][4]
                descriptor(name, landed, landed, dev_sib).wait_recv()

    def send(name):
        needs, source, target, device, _ = sends[name]
        arrive(needs)
        descriptor(name, source, target, device).start()

    def send_half(when, source):
        @pl.when(when)
        def _():
            descriptor("half", source, slot(HALF), dev_zo).start()

    col = lax.broadcasted_iota(jnp.int32, (rows, 512), 1)
    lane_sign = jnp.where(col < 256, 1.0, -1.0) * jnp.where(x < 2, 1.0, -1.0)

    def prepare(u):
        loads[u].wait()
        start = pl.multiple_of(blocks[u] * rows, rows)
        re = mats[u, 0, pl.ds(start, rows), :].astype(jnp.float32) * lane_sign
        im = mats[u, 1, pl.ds(start, rows), :].astype(jnp.float32) * lane_sign
        left[0, u, 0] = re.astype(jnp.bfloat16)
        left[0, u, 1] = (-im).astype(jnp.bfloat16)
        left[1, u, 0] = im.astype(jnp.bfloat16)
        left[1, u, 1] = re.astype(jnp.bfloat16)

    def sink_product(u):
        if u == 0:
            start = pl.multiple_of(snk * rows, rows)
            er = full[:, 0, pl.ds(start, rows), :]
            ei = full[:, 1, pl.ds(start, rows), :]
        else:
            er = other[slots[u], :, 0]
            ei = other[slots[u], :, 1]
        e = jnp.concatenate(
            [er.reshape(ops * rows, 512), ei.reshape(ops * rows, 512)], axis=1
        )
        pr = mats[u, 0]
        pi = mats[u, 1]
        re = dot(e, jnp.concatenate([pr, -pi], axis=0))
        xs[u, 0] = re.astype(jnp.bfloat16).reshape(ops, rows, 512)
        im = dot(e, jnp.concatenate([pi, pr], axis=0))
        xs[u, 1] = im.astype(jnp.bfloat16).reshape(ops, rows, 512)

    lane = lax.broadcasted_iota(jnp.int32, (384, 128), 1)

    def source_product(px, pyh, first, groups):
        cols = pl.ds(pl.multiple_of(px * 128, 128), 128)
        krows = pl.ds(pl.multiple_of((px * 2 + pyh) * rows, rows), rows)
        here = (lane // 64) == pyh
        for m in range(3):
            units = slice(3 * m, 3 * m + 3)
            a = jnp.concatenate(
                [left[0, units].reshape(384, 512), left[1, units].reshape(384, 512)], axis=1
            )
            for q in groups:
                w = jnp.concatenate(
                    [full[4 * q : 4 * q + 4, c, krows, :].reshape(256, 512) for c in range(2)],
                    axis=1,
                )
                r = dot_nt(a, w)
                for j in range(2):
                    v = r[:, 128 * j : 128 * j + 128]
                    t = pltpu.roll(v, 64, 1)
                    for k, new in enumerate(
                        (jnp.where(lane < 64, v, t), jnp.where(lane < 64, t, v))
                    ):
                        o = q * 4 + 2 * j + k
                        new = new.astype(jnp.bfloat16)
                        if not first:
                            new = jnp.where(here, new, ys[units, :, o, :, cols].reshape(384, 128))
                        ys[units, :, o, :, cols] = new.reshape(3, 2, rows, 128)

    r_iota = lax.broadcasted_iota(jnp.int32, (256, 256), 0)
    c_iota = lax.broadcasted_iota(jnp.int32, (256, 256), 1)
    same = lax.rem(r_iota, 16) == lax.rem(c_iota, 16)

    def trace(columns, units, last):
        for u in units:
            total = dot_nt(*(
                jnp.concatenate(
                    [
                        held[u, :, :, 16 * i : 16 * i + 16,
                             pl.ds(pl.multiple_of(px * 128, 128), 128)].reshape(256, 128)
                        for i in range(rows // 16)
                        for px in columns
                    ],
                    axis=1,
                )
                for held in (xs, ys)
            ))
            if last:
                total = jnp.where(same, total + gram[u], 0.0)
                rowed[u] = jnp.sum(total.reshape(2 * ops, 16, 256), axis=1)
            else:
                gram[u] = total

    sinks = (
        (), ("sib",), flips + ("sib_flip",), ("next",), ("sib_next",), prevs, ("sib_prev",),
        ("half",), ("sib_half",),
    )
    both = (0, 1)
    products = {
        "Yx1": (x, yhi, both, ()),
        "Yx2": (x, yoh, both, partners),
        "Yb1": (xb, yhi, both, ("fore_tail", "fore_fifth", "fore_head")),
        "Yf1": (xf, yhi, both, ("back_tail", "back_fifth", "back_head")),
        "Yo1": (xo, yhi, both, ("pass_tail", "pass_fifth", "pass_head")),
        "Yb2u": (xb, yoh, (1,), ("fore_triple", "cross_b")),
        "Yb2l": (xb, yoh, (0,), ("fore_pair", "fore_triple")),
        "Yf2u": (xf, yoh, (1,), ("back_triple", "cross_f")),
        "Yf2l": (xf, yoh, (0,), ("back_pair", "back_triple")),
        "Yo2u": (xo, yoh, (1,), ("cross_o", "cross_o5")),
        "Yo2l": (xo, yoh, (0,), ("pass_pair", "pass_twin")),
    }
    for name in ORDER:
        if name in sends:
            send(name)
        elif name == "half_own":
            send_half(jnp.logical_not(low), mine())
        elif name == "half_flip":
            arrive(flips)
            send_half(low, slot(FLIP))
        elif name in products:
            px, pyh, groups, needs = products[name]
            arrive(needs)
            source_product(px, pyh, name[2] == "1", groups)
        elif name[0] == "S":
            if name == "S0":
                own_load.wait()
                for u in range(UNITS):
                    prepare(u)
            u = int(name[1])
            arrive(sinks[u])
            sink_product(u)
        elif name == "T1a":
            trace((x, xf), range(7), False)
        elif name == "T1b":
            trace((x, xf), range(7, UNITS), False)
        else:
            trace((xb, xo), range(UNITS), True)

    parts[...] = jnp.zeros_like(parts)
    pick_row = lax.broadcasted_iota(jnp.int32, (16, 256), 0)
    pick_group = lax.broadcasted_iota(jnp.int32, (16, 256), 1) // 16
    straight = jnp.where(pick_row == pick_group, 1.0, 0.0)
    crossed = jnp.where(
        pick_row < 8,
        jnp.where(pick_group == pick_row + 8, -1.0, 0.0),
        jnp.where(pick_group == pick_row - 8, 1.0, 0.0),
    )
    traces = exact_nt(rowed[:, 0:8].reshape(UNITS * 8, 256), straight) + exact_nt(
        rowed[:, 8:16].reshape(UNITS * 8, 256), crossed
    )
    for u in range(UNITS):
        parts[taus[u], cores[u], :, 0:16] = traces[8 * u : 8 * u + 8]

    swap_copies = []
    for u in range(2, UNITS):
        copy = pltpu.make_async_remote_copy(
            src_ref=parts.at[taus[u], cores[u]], dst_ref=swapped.at[core, snk],
            send_sem=swap_send.at[u - 2], recv_sem=swap_recv.at[core, snk],
            device_id=(taus[u] * 2 + cores[u], tau), device_id_type=MESH,
        )
        copy.start()
        swap_copies.append(copy)
    part_copies = []
    for step in range(1, 8):
        to = lax.rem(snk + step, 8)
        copy = pltpu.make_async_remote_copy(
            src_ref=parts.at[to], dst_ref=sums.at[step], send_sem=part_send.at[step],
            recv_sem=part_recv.at[step], device_id=(src, to), device_id_type=MESH,
        )
        copy.start()
        part_copies.append(copy)
    sums[0] = parts[snk]
    for copy in part_copies:
        copy.wait()
    for c in range(2):
        @pl.when(jnp.logical_not(computed(c)))
        def _(c=c):
            for k in range(8):
                pltpu.make_async_remote_copy(
                    src_ref=swapped.at[c, k], dst_ref=swapped.at[c, k],
                    send_sem=swap_send.at[0], recv_sem=swap_recv.at[c, k],
                    device_id=dev_sib, device_id_type=MESH,
                ).wait_recv()
    for copy in swap_copies:
        copy.wait_send()

    turn_row = lax.broadcasted_iota(jnp.int32, (8, 128), 0)
    turn_lane = lax.broadcasted_iota(jnp.int32, (8, 128), 1)
    for c in range(2):
        total = jnp.sum(sums[:, c], axis=0)
        other_total = jnp.sum(swapped[c], axis=0)
        for part in range(2):
            turn = jnp.where(turn_lane == turn_row + 8 * part, 1.0, 0.0)
            out[part, 0, c] = total[:, 8 * part : 8 * part + 8] + exact_nt(turn, other_total)
    for name, (_, source, target, device, _) in sends.items():
        descriptor(name, source, target, device).wait_send()


def on_device(perambulators, elements):
    ops, rows, width = elements.shape[1], elements.shape[3], elements.shape[4]
    bf16, f32 = jnp.bfloat16, jnp.float32
    copies = 48
    return pl.pallas_call(
        kernel,
        out_shape=jax.ShapeDtypeStruct((2, 1, 2, ops, ops), f32),
        in_specs=[pl.BlockSpec(memory_space=pl.ANY)] * 2,
        out_specs=pl.BlockSpec(memory_space=pltpu.VMEM),
        scratch_shapes=[
            pltpu.VMEM((ops, 2, width, width), bf16),
            pltpu.VMEM((9, ops, 2, rows, width), bf16),
            pltpu.VMEM((UNITS, 2, width, width), bf16),
            pltpu.VMEM((2, UNITS, 2, rows, width), bf16),
            pltpu.VMEM((UNITS, 2, ops, rows, width), bf16),
            pltpu.VMEM((UNITS, 2, ops, rows, width), bf16),
            pltpu.VMEM((UNITS, 256, 256), f32),
            pltpu.VMEM((UNITS, 16, 256), f32),
            pltpu.VMEM((8, 2, 8, 128), f32),
            pltpu.VMEM((8, 2, 8, 128), f32),
            pltpu.VMEM((2, 8, 8, 128), f32),
            pltpu.SemaphoreType.DMA((UNITS + 1,)),
            pltpu.SemaphoreType.DMA((copies,)),
            pltpu.SemaphoreType.DMA((copies,)),
            pltpu.SemaphoreType.DMA((8,)),
            pltpu.SemaphoreType.DMA((8,)),
            pltpu.SemaphoreType.DMA((UNITS - 2,)),
            pltpu.SemaphoreType.DMA((2, 8)),
        ],
        compiler_params=pltpu.CompilerParams(
            collective_id=0, has_side_effects=True, vmem_limit_bytes=62 * 2**20
        ),
        cost_estimate=pl.CostEstimate(
            flops=20 * 10**9, bytes_accessed=12 * 2**20, transcendentals=0
        ),
        name="correlate",
    )(perambulators, elements)


def solution(mesh):
    placed = (P("src", None, None, None, None), P("src", None, None, "snk", None))
    return jax.shard_map(
        on_device,
        mesh=mesh,
        in_specs=placed,
        out_specs=P(None, "src", "snk", None, None),
        check_vma=False,
    )
```
